32 devices in a mesh: rep: 4 (over z), table: 4 (over y, core), tensor: 2 (over x).
Axes of the slice: x: 2, y: 2, z: 4, core: 2. Of those that a mesh axis runs over, the one named last changes fastest.
Arguments:
- pooled: bfloat16 [128, 256, 192], P('rep', 'table'), may hold values from -6 to 6
- lc_weight: bfloat16 [256, 256], P('tensor'), may hold values from -0.375 to 0.375
- fm_proj: bfloat16 [256, 256], P(None, 'tensor'), may hold values from -0.375 to 0.375
- fm_out: bfloat16 [256, 192], P('tensor'), may hold values from -0.02734375 to 0.02734375
- cotangent: bfloat16 [128, 256, 192], P(('rep', 'table')), may hold values from -6 to 6
Outputs:
- layer_out: bfloat16 [128, 256, 192], P(('rep', 'table'))
- emb_grad: bfloat16 [128, 256, 192], P('rep', 'table', 'tensor')
- lc_grad: float32 [256, 256], P('tensor')
- proj_grad: float32 [256, 256], P(None, 'tensor')
- out_grad: float32 [256, 192], P('tensor')
The draws below stay inside these ranges and needn't reach their ends.
All inputs are finite; a program needn't handle non-finite values.
Results may differ from the reference program's by a relative error of at most 0.015.
Values may be sent and summed in bfloat16 or wider, within the bound.
A program may use at most 64 MiB of HBM per device.

```python
import jax
import jax.numpy as jnp
from jax import lax

NEMB = 256
D = 192
K = 256
SAMP = 8
BATCH = 128
N_TENSOR = 2


def steps_of(key, dims, pieces, smallest, largest):
    factor_of = 1.0
    for axis_at, shards_of in pieces:
        steps = jax.random.uniform(jax.random.fold_in(jax.random.fold_in(key, 6), axis_at), (shards_of,), jnp.float32, smallest / len(pieces), largest / len(pieces))
        factor_of = factor_of * jnp.repeat(jnp.exp(steps), dims[axis_at] // shards_of).reshape((-1,) + (1,) * (len(dims) - 1 - axis_at))
    return factor_of


def bell_draw(stream_key, dims, width, bound, split=(), kind=jnp.bfloat16):
    entries = width * jax.random.normal(stream_key, dims, jnp.float32)
    if split:
        entries = entries * steps_of(stream_key, dims, split, -0.22, 0.18)
    return jnp.clip(entries, -bound, bound).astype(kind)


def setup_inputs(seed: int = 0) -> dict:
    splits = jax.random.split(jax.random.key(seed), 6)
    return {
        "pooled": bell_draw(splits[0], (BATCH, NEMB, D), 1.0, 6.0, ((0, 4), (1, 4))),
        "lc_weight": bell_draw(splits[1], (NEMB, NEMB), NEMB ** -0.5, 0.375, ((0, 2),)),
        "fm_proj": bell_draw(splits[2], (NEMB, K), NEMB ** -0.5, 0.375, ((1, 2),)),
        "fm_out": bell_draw(splits[3], (K, D), (K * D) ** -0.5, 0.02734375, ((0, 2),)),
        "cotangent": bell_draw(splits[4], (BATCH, NEMB, D), 1.0, 6.0, ((0, 16),)),
    }


def quarter_terms(embeds, upstream, proj_part, out_part, lc_part, row_start):
    row_count = lc_part.shape[0]
    embeds_wide = embeds.astype(jnp.float32)
    upstream_wide = upstream.astype(jnp.float32)
    compressed = jnp.einsum('snd,nk->sdk', embeds_wide, proj_part.astype(jnp.float32)).astype(jnp.bfloat16)
    interact = jnp.einsum('snd,sdk->snk', embeds_wide, compressed.astype(jnp.float32)).astype(jnp.bfloat16)
    own_rows = embeds_wide[:, row_start:row_start + row_count]
    forward_term = jnp.einsum('snk,kd->snd', interact.astype(jnp.float32), out_part.astype(jnp.float32))
    forward_term = forward_term + jnp.einsum('sjd,jm->smd', own_rows, lc_part.astype(jnp.float32))
    interact_grad = jnp.einsum('snd,kd->snk', upstream_wide, out_part.astype(jnp.float32)).astype(jnp.bfloat16)
    compress_grad = jnp.einsum('snd,snk->sdk', embeds_wide, interact_grad.astype(jnp.float32)).astype(jnp.bfloat16)
    input_grad = jnp.einsum('snk,sdk->snd', interact_grad.astype(jnp.float32), compressed.astype(jnp.float32))
    input_grad = input_grad + jnp.einsum('nk,sdk->snd', proj_part.astype(jnp.float32), compress_grad.astype(jnp.float32))
    lc_rows = jnp.einsum('jm,smd->sjd', lc_part.astype(jnp.float32), upstream_wide) + upstream_wide[:, row_start:row_start + row_count]
    input_grad = input_grad.at[:, row_start:row_start + row_count].add(lc_rows)
    out_term = jnp.einsum('snk,snd->kd', interact.astype(jnp.float32), upstream_wide)
    proj_term = jnp.einsum('snd,sdk->nk', embeds_wide, compress_grad.astype(jnp.float32))
    lc_term = jnp.einsum('sjd,smd->jm', own_rows, upstream_wide)
    return forward_term, input_grad, out_term, proj_term, lc_term


def reference(pooled, lc_weight, fm_proj, fm_out, cotangent):
    key_count = K // N_TENSOR
    row_count = NEMB // N_TENSOR
    block_total = BATCH // SAMP
    embed_blocks = pooled.reshape(block_total, SAMP, NEMB, D)
    upstream_blocks = cotangent.reshape(block_total, SAMP, NEMB, D)

    def sample_step(totals, sample_pair):
        embeds, upstream = sample_pair
        mixture = jnp.zeros((SAMP, NEMB, D), jnp.float32)
        input_grad = jnp.zeros((SAMP, NEMB, D), jnp.float32)
        out_blocks = []
        proj_blocks = []
        lc_blocks = []
        for segment in range(N_TENSOR):
            keys = slice(segment * key_count, (segment + 1) * key_count)
            rows = slice(segment * row_count, (segment + 1) * row_count)
            block_terms = quarter_terms(embeds, upstream, fm_proj[:, keys], fm_out[keys], lc_weight[rows], segment * row_count)
            mixture = mixture + lax.optimization_barrier(block_terms[0].astype(jnp.bfloat16)).astype(jnp.float32)
            input_grad = input_grad + block_terms[1]
            out_blocks.append(block_terms[2])
            proj_blocks.append(block_terms[3])
            lc_blocks.append(block_terms[4])
        layer_rows = (embeds.astype(jnp.float32) + mixture).astype(jnp.bfloat16)
        totals = (totals[0] + jnp.concatenate(out_blocks, 0),
                  totals[1] + jnp.concatenate(proj_blocks, 1),
                  totals[2] + jnp.concatenate(lc_blocks, 0))
        return totals, (layer_rows, input_grad.astype(jnp.bfloat16))

    start_totals = (jnp.zeros((K, D), jnp.float32), jnp.zeros((NEMB, K), jnp.float32), jnp.zeros((NEMB, NEMB), jnp.float32))
    totals, stacked = lax.scan(sample_step, start_totals, (embed_blocks, upstream_blocks))
    wide_scale = float(BATCH * D) ** -0.5
    out_scale = float(BATCH * NEMB * D) ** -0.5
    layer_out = stacked[0].reshape(BATCH, NEMB, D)
    emb_grad = stacked[1].reshape(BATCH, NEMB, D)
    return (layer_out, emb_grad, totals[2] * wide_scale, totals[1] * wide_scale, totals[0] * out_scale)
```

```python
import functools

import jax
import jax.numpy as jnp
from jax import lax
from jax.experimental import pallas as pl
from jax.experimental.pallas import tpu as pltpu
from jax.sharding import PartitionSpec as P

MESH = pl.DeviceIdType.MESH
BF16 = jnp.bfloat16
F32 = jnp.float32


def dot_nn(a, b):
    return jnp.dot(a, b, preferred_element_type=F32)


def dot_nt(a, b):
    return lax.dot_general(a, b, (((1,), (1,)), ((), ())), preferred_element_type=F32)


def layer_kernel(cfg, pooled, lc_w, proj_w, out_w, cot, layer, emb, lc_g, proj_g, out_g, *scratch):
    (x_ref, g_ref, pw, ww, ow, pt, p_all, w_t, ct, cgt, lo, eg, acc_l, acc_p, acc_o,
     gb, rb1, sb, rb2, fs, loc, x_send, x_recv, w_send, w_recv, e_send, e_recv, r_send, r_recv) = scratch
    tables, reps, tensors = cfg["tables"], cfg["reps"], cfg["tensors"]
    samples, nr, n, d = cfg["samples"], cfg["nr"], cfg["n"], cfg["d"]
    kq, jq, dq, cs, pp, fused = cfg["kq"], cfg["jq"], cfg["dq"], cfg["cs"], cfg["pp"], cfg["fused"]
    chunks = samples // cs
    t = lax.axis_index("table")
    r = lax.axis_index("rep")
    x = lax.axis_index("tensor")

    def peer(axis, me, size, j):
        return {axis: lax.rem(me + j, size)}

    barrier = pltpu.get_barrier_semaphore()
    groups = [("table", t, tables), ("tensor", x, tensors)] + ([("rep", r, reps)] if fused else [])
    signals = 0
    for axis, me, size in groups:
        for j in range(1, size):
            pl.semaphore_signal(barrier, inc=1, device_id=peer(axis, me, size, j), device_id_type=MESH)
            signals += 1

    def g_load(c):
        rows = pl.ds(c * cs, cs)
        return pltpu.make_async_copy(cot.at[rows], g_ref.at[rows], loc.at[c])

    def x_load(c):
        return pltpu.make_async_copy(
            pooled.at[pl.ds(t * samples + c * cs, cs)], x_ref.at[pl.ds(c * cs, cs), t], loc.at[chunks + c]
        )

    w_pairs = ((proj_w, pw), (out_w, ow), (lc_w, ww))
    w_loads = [
        pltpu.make_async_copy(src, dst.at[x], loc.at[2 * chunks + i]) for i, (src, dst) in enumerate(w_pairs)
    ]
    for load in w_loads:
        load.start()
    for c in range(chunks):
        g_load(c).start()
        x_load(c).start()
    pl.semaphore_wait(barrier, signals)

    def x_copy(c, j):
        to = lax.rem(t + j, tables)
        return pltpu.make_async_remote_copy(
            pooled.at[pl.ds(to * samples + c * cs, cs)],
            x_ref.at[pl.ds(c * cs, cs), t],
            x_send.at[c, j - 1],
            x_recv.at[c, j - 1],
            device_id=peer("table", t, tables, j),
            device_id_type=MESH,
        )

    def w_copy(i, j):
        src, dst = w_pairs[i]
        return pltpu.make_async_remote_copy(
            src, dst.at[x], w_send.at[i, j - 1], w_recv.at[i, j - 1],
            device_id=peer("tensor", x, tensors, j), device_id_type=MESH,
        )

    for c in range(chunks):
        for j in range(1, tables):
            x_copy(c, j).start()
    for j in range(1, tensors):
        for i in range(3):
            w_copy(i, j).start()

    for load in w_loads:
        load.wait()
    pt[x] = pw[x].T
    acc_l[...] = jnp.zeros_like(acc_l)
    acc_p[...] = jnp.zeros_like(acc_p)
    acc_o[...] = jnp.zeros_like(acc_o)

    def first(c, carry):
        g_load(c).wait()
        x_load(c).wait()
        for j in range(1, tables):
            x_copy(c, j).wait_recv()
        own_pt, own_o = pt[x], ow[x]
        sum_l, sum_p, sum_o = acc_l[...], acc_p[...], acc_o[:, :d]
        for i in range(cs):
            s = c * cs + i
            xs = x_ref[s].reshape(n, d)
            gs = g_ref[s]
            own_rows = x_ref[s, pl.ds(x * (jq // nr), jq // nr)].reshape(jq, d)
            comp = dot_nn(own_pt, xs).astype(BF16)
            ct[s, x] = comp
            inter = dot_nt(comp, xs).astype(BF16)
            sum_o = sum_o + dot_nn(inter, gs)
            igrad = dot_nt(own_o, gs).astype(BF16)
            cgrad = dot_nn(igrad, xs).astype(BF16)
            cgt[s, x] = cgrad
            sum_p = sum_p + dot_nt(cgrad, xs)
            sum_l = sum_l + dot_nt(own_rows, gs)
        acc_l[...] = sum_l
        acc_p[...] = sum_p
        acc_o[:, :d] = sum_o
        return carry

    lax.fori_loop(0, chunks, first, 0)

    part = reps * pp

    def rs_table(j):
        to = lax.rem(t + j, tables)
        return pltpu.make_async_remote_copy(
            gb.at[pl.ds(to * part, part)], rb1.at[j - 1], r_send.at[0, j - 1], r_recv.at[0, j - 1],
            device_id=peer("table", t, tables, j), device_id_type=MESH,
        )

    def rs_rep(j):
        to = lax.rem(r + j, reps)
        return pltpu.make_async_remote_copy(
            sb.at[pl.ds(to * pp, pp)], rb2.at[j - 1], r_send.at[1, j - 1], r_recv.at[1, j - 1],
            device_id=peer("rep", r, reps, j), device_id_type=MESH,
        )

    def ag_rep(j):
        mine = fs.at[pl.ds(t * part + r * pp, pp)]
        return pltpu.make_async_remote_copy(
            mine, mine, r_send.at[2, j - 1], r_recv.at[2, j - 1],
            device_id=peer("rep", r, reps, j), device_id_type=MESH,
        )

    def ag_table(j):
        mine = fs.at[pl.ds(t * part, part)]
        return pltpu.make_async_remote_copy(
            mine, mine, r_send.at[3, j - 1], r_recv.at[3, j - 1],
            device_id=peer("table", t, tables, j), device_id_type=MESH,
        )

    halves = n // 128
    layout = ((acc_l, jq, cfg["wide_scale"]), (acc_p, kq, cfg["wide_scale"]), (acc_o, kq, cfg["out_scale"]))
    if fused:
        at = 0
        for ref, rows, scale in layout:
            for h in range(halves):
                value = (ref[:, h * 128:(h + 1) * 128] * scale).astype(BF16)
                gb[at:at + rows // 16] = value.reshape(rows // 16, 16, 128)
                at += rows // 16
        for j in range(1, tables):
            rs_table(j).start()

    def reduce_step(c):
        if not fused:
            return

        @pl.when(c == 0)
        def _():
            total = gb[pl.ds(t * part, part)].astype(F32)
            for j in range(1, tables):
                rs_table(j).wait_recv()
                total = total + rb1[j - 1].astype(F32)
            sb[...] = total.astype(BF16)
            for j in range(1, reps):
                rs_rep(j).start()

        @pl.when(c == 1)
        def _():
            total = sb[pl.ds(r * pp, pp)].astype(F32)
            for j in range(1, reps):
                rs_rep(j).wait_recv()
                total = total + rb2[j - 1].astype(F32)
            fs[pl.ds(t * part + r * pp, pp)] = total.astype(BF16)
            for j in range(1, reps):
                ag_rep(j).start()

        @pl.when(c == 2)
        def _():
            for j in range(1, reps):
                ag_rep(j).wait_recv()
            for j in range(1, tables):
                ag_table(j).start()

    for j in range(1, tensors):
        for i in range(3):
            w_copy(i, j).wait_recv()
    for j in range(1, tensors):
        q = lax.rem(x + j, tensors)
        pt[q] = pw[q].T
    p_all[...] = jnp.concatenate([pw[q] for q in range(tensors)], axis=1)
    w_t[...] = ww[...].reshape(n, n).T

    def lo_store(c):
        rows = pl.ds(c * cs, cs)
        return pltpu.make_async_copy(lo.at[rows], layer.at[rows], loc.at[2 * chunks + 3 + c])

    def e_store(c):
        return pltpu.make_async_copy(
            eg.at[pl.ds(c * cs, cs), t], emb.at[pl.ds(t * samples + c * cs, cs)], loc.at[3 * chunks + 3 + c]
        )

    def e_copy(c, j):
        to = lax.rem(t + j, tables)
        return pltpu.make_async_remote_copy(
            eg.at[pl.ds(c * cs, cs), to],
            emb.at[pl.ds(t * samples + c * cs, cs)],
            e_send.at[c, j - 1],
            e_recv.at[c, j - 1],
            device_id=peer("table", t, tables, j),
            device_id_type=MESH,
        )

    def second(c, carry):
        o_all = ow[...].reshape(tensors * kq, d)
        for i in range(cs):
            s = c * cs + i
            xs = x_ref[s].reshape(n, d)
            gs = g_ref[s]
            for j in range(1, tensors):
                q = lax.rem(x + j, tensors)
                ct[s, q] = dot_nn(pt[q], xs).astype(BF16)
                igrad_t = dot_nt(ow[q], gs).astype(BF16)
                cgt[s, q] = dot_nn(igrad_t, xs).astype(BF16)
            comp = ct[s].reshape(tensors * kq, d)
            cgrad = cgt[s].reshape(tensors * kq, d)
            igrad = dot_nt(gs, o_all).astype(BF16)
            grad = dot_nn(igrad, comp) + dot_nn(p_all[...], cgrad)
            grad = grad + dot_nn(ww[...].reshape(n, n), gs) + gs.astype(F32)
            own = grad[:, :dq]
            for q in range(1, tensors):
                own = jnp.where(x == q, grad[:, q * dq:(q + 1) * dq], own)
            eg[s] = own.reshape(tables, nr, dq).astype(BF16)
            inter = dot_nt(xs, comp).astype(BF16)
            mixture = dot_nn(inter, o_all) + dot_nn(w_t[...], xs)
            lo[s] = (xs.astype(F32) + mixture).astype(BF16)
        for j in range(1, tables):
            e_copy(c, j).start()
        e_store(c).start()
        lo_store(c).start()
        reduce_step(c)
        return carry

    lax.fori_loop(0, chunks, second, 0)

    if fused:
        for j in range(1, tables):
            ag_table(j).wait_recv()
        at = 0
        wide = []
        for ref, rows, scale in layout:
            pieces = []
            for h in range(halves):
                pieces.append(fs[at:at + rows // 16].reshape(rows, 128).astype(F32))
                at += rows // 16
            wide.append(pieces)
        lc_g[...] = jnp.concatenate(wide[0], axis=1)
        proj_g[...] = jnp.concatenate([piece.T for piece in wide[1]], axis=0)
        out_g[...] = jnp.concatenate(wide[2], axis=1)[:, :d]
    else:
        lc_g[...] = acc_l[...] * cfg["wide_scale"]
        proj_g[...] = (acc_p[...] * cfg["wide_scale"]).T
        out_g[...] = acc_o[:, :d] * cfg["out_scale"]

    for c in range(chunks):
        lo_store(c).wait()
        e_store(c).wait()
        for j in range(1, tables):
            e_copy(c, j).wait_recv()
    for c in range(chunks):
        for j in range(1, tables):
            x_copy(c, j).wait_send()
            e_copy(c, j).wait_send()
    for j in range(1, tensors):
        for i in range(3):
            w_copy(i, j).wait_send()
    if fused:
        for j in range(1, tables):
            rs_table(j).wait_send()
            ag_table(j).wait_send()
        for j in range(1, reps):
            rs_rep(j).wait_send()
            ag_rep(j).wait_send()


def shards(sizes, pooled, lc_weight, fm_proj, fm_out, cotangent):
    tables, reps, tensors = sizes["table"], sizes["rep"], sizes["tensor"]
    samples, n, d = cotangent.shape
    nr = pooled.shape[1]
    jq, kq, dq = lc_weight.shape[0], fm_out.shape[0], d // tensors
    total = samples * reps * tables
    cs = 2 if samples % 2 == 0 else 1
    chunks = samples // cs
    wide = -(-d // 128) * 128
    pieces = (n // 128) * (jq // 16 + kq // 16) + (wide // 128) * (kq // 16)
    group = tables * reps
    fused = pieces % group == 0 and wide == n and jq % 16 == 0 and kq % 16 == 0
    pp = pieces // group if fused else 1
    cfg = dict(
        tables=tables, reps=reps, tensors=tensors, samples=samples, nr=nr, n=n, d=d, kq=kq, jq=jq, dq=dq,
        cs=cs, pp=pp, fused=fused,
        wide_scale=float(total * d) ** (-0.5), out_scale=float(total * n * d) ** (-0.5),
    )
    part = reps * pp if fused else 1
    held = pieces if fused else 1
    dma = pltpu.SemaphoreType.DMA
    peers = max(tables - 1, 1)
    wpeers = max(tensors - 1, 1)
    rpeers = max(tables - 1, reps - 1, 1)
    scratch = [
        pltpu.VMEM((samples, tables, nr, d), BF16),
        pltpu.VMEM((samples, n, d), BF16),
        pltpu.VMEM((tensors, n, kq), BF16),
        pltpu.VMEM((tensors, jq, n), BF16),
        pltpu.VMEM((tensors, kq, d), BF16),
        pltpu.VMEM((tensors, kq, n), BF16),
        pltpu.VMEM((n, tensors * kq), BF16),
        pltpu.VMEM((n, n), BF16),
        pltpu.VMEM((samples, tensors, kq, d), BF16),
        pltpu.VMEM((samples, tensors, kq, d), BF16),
        pltpu.VMEM((samples, n, d), BF16),
        pltpu.VMEM((samples, tables, nr, dq), BF16),
        pltpu.VMEM((jq, n), F32),
        pltpu.VMEM((kq, n), F32),
        pltpu.VMEM((kq, wide), F32),
        pltpu.VMEM((held, 16, 128), BF16),
        pltpu.VMEM((peers, part, 16, 128), BF16),
        pltpu.VMEM((part, 16, 128), BF16),
        pltpu.VMEM((max(reps - 1, 1), pp, 16, 128), BF16),
        pltpu.VMEM((held, 16, 128), BF16),
        dma((4 * chunks + 3,)),
        dma((chunks, peers)),
        dma((chunks, peers)),
        dma((3, wpeers)),
        dma((3, wpeers)),
        dma((chunks, peers)),
        dma((chunks, peers)),
        dma((4, rpeers)),
        dma((4, rpeers)),
    ]
    hbm = pl.BlockSpec(memory_space=pl.ANY)
    vmem = pl.BlockSpec(memory_space=pltpu.VMEM)
    layer, emb, lc_g, proj_g, out_g = pl.pallas_call(
        functools.partial(layer_kernel, cfg),
        out_shape=(
            jax.ShapeDtypeStruct((samples, n, d), BF16),
            jax.ShapeDtypeStruct((pooled.shape[0], nr, dq), BF16),
            jax.ShapeDtypeStruct((jq, n), F32),
            jax.ShapeDtypeStruct((n, kq), F32),
            jax.ShapeDtypeStruct((kq, d), F32),
        ),
        in_specs=[hbm] * 5,
        out_specs=(hbm, hbm, vmem, vmem, vmem),
        scratch_shapes=scratch,
        compiler_params=pltpu.CompilerParams(
            collective_id=0, has_side_effects=True, vmem_limit_bytes=48 * 1024 * 1024
        ),
        name="interaction_layer",
    )(pooled, lc_weight, fm_proj, fm_out, cotangent)
    if not fused:
        lc_g, proj_g, out_g = lax.psum((lc_g, proj_g, out_g), ("rep", "table"))
    return layer, emb, lc_g, proj_g, out_g


def solution(mesh):
    in_specs = (
        P("rep", "table", None),
        P("tensor", None),
        P(None, "tensor"),
        P("tensor", None),
        P(("rep", "table"), None, None),
    )
    out_specs = (
        P(("rep", "table"), None, None),
        P("rep", "table", "tensor"),
        P("tensor", None),
        P(None, "tensor"),
        P("tensor", None),
    )
    return jax.shard_map(
        functools.partial(shards, dict(mesh.shape)),
        mesh=mesh, in_specs=in_specs, out_specs=out_specs, check_vma=False,
    )
```

```python
import functools

import jax
import jax.numpy as jnp
from jax import lax
from jax.experimental import pallas as pl
from jax.experimental.pallas import tpu as pltpu
from jax.sharding import PartitionSpec as P

MESH = pl.DeviceIdType.MESH
BF16 = jnp.bfloat16
F32 = jnp.float32
VMEM_BYTES = 60 * 1024 * 1024


def dot_nn(a, b):
    return jnp.dot(a, b, preferred_element_type=F32)


def layer_kernel(cfg, pooled, lc_w, proj_w, out_w, cot, layer, emb, *rest):
    tables, reps, tensors = cfg["tables"], cfg["reps"], cfg["tensors"]
    samples, nr, n, d = cfg["samples"], cfg["nr"], cfg["n"], cfg["d"]
    kq, jq, dq, cs, pp, fused = cfg["kq"], cfg["jq"], cfg["dq"], cfg["cs"], cfg["pp"], cfg["fused"]
    k = kq * tensors
    grads, scratch = (rest[:1], rest[1:]) if fused else (rest[:3], rest[3:])
    (x_ref, gt_ref, pw, ww, ow, pt, lhs, rhs, f_lhs, f_rhs, igt, lo, eg, acc_l, acc_p, acc_o,
     gb, rb1, sb, rb2, fs, loc, x_send, x_recv, w_send, w_recv, e_send, e_recv, r_send, r_recv) = scratch
    chunks = samples // cs
    t = lax.axis_index("table")
    r = lax.axis_index("rep")
    x = lax.axis_index("tensor")

    def peer(axis, me, size, j):
        return {axis: lax.rem(me + j, size)}

    barrier = pltpu.get_barrier_semaphore()
    groups = [("table", t, tables), ("tensor", x, tensors)] + ([("rep", r, reps)] if fused else [])
    signals = 0
    for axis, me, size in groups:
        for j in range(1, size):
            pl.semaphore_signal(barrier, inc=1, device_id=peer(axis, me, size, j), device_id_type=MESH)
            signals += 1

    g_load = pltpu.make_async_copy(cot, gt_ref, loc.at[chunks])

    def x_load(c):
        return pltpu.make_async_copy(
            pooled.at[pl.ds(t * samples + c * cs, cs)], x_ref.at[pl.ds(c * cs, cs), t], loc.at[c]
        )

    w_pairs = ((proj_w, pw), (out_w, ow), (lc_w, ww))
    w_loads = [
        pltpu.make_async_copy(src, dst.at[x], loc.at[chunks + 1 + i]) for i, (src, dst) in enumerate(w_pairs)
    ]
    for load in w_loads:
        load.start()
    g_load.start()
    for c in range(chunks):
        x_load(c).start()
    pl.semaphore_wait(barrier, signals)

    def x_copy(c, j):
        to = lax.rem(t + j, tables)
        return pltpu.make_async_remote_copy(
            pooled.at[pl.ds(to * samples + c * cs, cs)],
            x_ref.at[pl.ds(c * cs, cs), t],
            x_send.at[c, j - 1],
            x_recv.at[c, j - 1],
            device_id=peer("table", t, tables, j),
            device_id_type=MESH,
        )

    def w_copy(i, j):
        src, dst = w_pairs[i]
        return pltpu.make_async_remote_copy(
            src, dst.at[x], w_send.at[i, j - 1], w_recv.at[i, j - 1],
            device_id=peer("tensor", x, tensors, j), device_id_type=MESH,
        )

    for c in range(chunks):
        for j in range(1, tables):
            x_copy(c, j).start()
    for j in range(1, tensors):
        for i in range(3):
            w_copy(i, j).start()

    for load in w_loads:
        load.wait()
    pt[x] = pw[x].T
    own_pt, own_o = pt[x], ow[x].T
    acc_l[...] = jnp.zeros_like(acc_l)
    acc_p[...] = jnp.zeros_like(acc_p)
    acc_o[...] = jnp.zeros_like(acc_o)
    g_load.wait()

    def block(q):
        return pl.ds(pl.multiple_of(q * kq, kq), kq)

    def before(c, carry):
        for i in range(cs):
            s = c * cs + i
            gt = gt_ref[s]
            rhs[s, 2 * k:] = gt.T
            igt[s] = dot_nn(own_o, gt).astype(BF16)
        return carry

    lax.fori_loop(0, chunks, before, 0)

    def first(c, carry):
        x_load(c).wait()
        for j in range(1, tables):
            x_copy(c, j).wait_recv()
        sum_l, sum_p, sum_o = acc_l[...], acc_p[...], acc_o[:, :d]
        for i in range(cs):
            s = c * cs + i
            xs = x_ref[s].reshape(n, d)
            own_rows = x_ref[s, pl.ds(x * (jq // nr), jq // nr)].reshape(jq, d)
            xt = xs.T
            f_lhs[s, :, k:] = xt
            cgrad = dot_nn(igt[s], xs).astype(BF16)
            rhs[s, pl.ds(pl.multiple_of(k + x * kq, kq), kq)] = cgrad
            comp = dot_nn(own_pt, xs).astype(BF16)
            rhs[s, block(x)] = comp
            inter = dot_nn(comp, xt).astype(BF16)
            f_rhs[s, block(x)] = inter
            sum_p = sum_p + dot_nn(cgrad, xt)
            sum_l = sum_l + dot_nn(own_rows, gt_ref[s])
            sum_o = sum_o + dot_nn(inter, rhs[s, 2 * k:])
        acc_l[...] = sum_l
        acc_p[...] = sum_p
        acc_o[:, :d] = sum_o
        return carry

    lax.fori_loop(0, chunks, first, 0)

    part = reps * pp

    def rs_table(j):
        to = lax.rem(t + j, tables)
        return pltpu.make_async_remote_copy(
            gb.at[pl.ds(to * part, part)], rb1.at[j - 1], r_send.at[0, j - 1], r_recv.at[0, j - 1],
            device_id=peer("table", t, tables, j), device_id_type=MESH,
        )

    def rs_rep(j):
        to = lax.rem(r + j, reps)
        return pltpu.make_async_remote_copy(
            sb.at[pl.ds(to * pp, pp)], rb2.at[j - 1], r_send.at[1, j - 1], r_recv.at[1, j - 1],
            device_id=peer("rep", r, reps, j), device_id_type=MESH,
        )

    def ag_rep(j):
        mine = fs.at[pl.ds(t * part + r * pp, pp)]
        return pltpu.make_async_remote_copy(
            mine, mine, r_send.at[2, j - 1], r_recv.at[2, j - 1],
            device_id=peer("rep", r, reps, j), device_id_type=MESH,
        )

    def ag_table(j):
        mine = fs.at[pl.ds(t * part, part)]
        return pltpu.make_async_remote_copy(
            mine, mine, r_send.at[3, j - 1], r_recv.at[3, j - 1],
            device_id=peer("table", t, tables, j), device_id_type=MESH,
        )

    layout = ((acc_l, jq, cfg["wide_scale"]), (acc_p, kq, cfg["wide_scale"]), (acc_o, kq, cfg["out_scale"]))
    if fused:
        at = 0
        for ref, rows, scale in layout:
            for h in range(n // 128):
                value = (ref[:, h * 128:(h + 1) * 128] * scale).astype(BF16)
                gb[at:at + rows // 16] = value.reshape(rows // 16, 16, 128)
                at += rows // 16
        for j in range(1, tables):
            rs_table(j).start()

    def reduce_step(c):
        if not fused:
            return

        @pl.when(c == 0)
        def _():
            total = gb[pl.ds(t * part, part)].astype(F32)
            for j in range(1, tables):
                rs_table(j).wait_recv()
                total = total + rb1[j - 1].astype(F32)
            sb[...] = total.astype(BF16)
            for j in range(1, reps):
                rs_rep(j).start()

        @pl.when(c == 1)
        def _():
            total = sb[pl.ds(r * pp, pp)].astype(F32)
            for j in range(1, reps):
                rs_rep(j).wait_recv()
                total = total + rb2[j - 1].astype(F32)
            fs[pl.ds(t * part + r * pp, pp)] = total.astype(BF16)
            for j in range(1, reps):
                ag_rep(j).start()

        @pl.when(c == 2)
        def _():
            for j in range(1, reps):
                ag_rep(j).wait_recv()
            for j in range(1, tables):
                ag_table(j).start()

    for j in range(1, tensors):
        for i in range(3):
            w_copy(i, j).wait_recv()
    for j in range(1, tensors):
        q = lax.rem(x + j, tensors)
        pt[q] = pw[q].T
    ot_all = jnp.concatenate([ow[q] for q in range(tensors)], axis=1)
    w_all = ww[...].reshape(n, n)
    for i in range(cs):
        lhs[i, :, k:2 * k] = jnp.concatenate([pw[q] for q in range(tensors)], axis=1)
        lhs[i, :, 2 * k:] = w_all
    for s in range(samples):
        f_lhs[s, :, :k] = ot_all
        f_rhs[s, k:] = w_all

    def lo_store(c):
        rows = pl.ds(c * cs, cs)
        return pltpu.make_async_copy(lo.at[rows], layer.at[rows], loc.at[chunks + 4 + c])

    def e_store(c):
        return pltpu.make_async_copy(
            eg.at[pl.ds(c * cs, cs), t], emb.at[pl.ds(t * samples + c * cs, cs)], loc.at[2 * chunks + 4 + c]
        )

    def e_copy(c, j):
        to = lax.rem(t + j, tables)
        return pltpu.make_async_remote_copy(
            eg.at[pl.ds(c * cs, cs), to],
            emb.at[pl.ds(t * samples + c * cs, cs)],
            e_send.at[c, j - 1],
            e_recv.at[c, j - 1],
            device_id=peer("table", t, tables, j),
            device_id_type=MESH,
        )

    def second(c, carry):
        for i in range(cs):
            s = c * cs + i
            xs = x_ref[s].reshape(n, d)
            xt = f_lhs[s, :, k:]
            gs = rhs[s, 2 * k:]
            for j in range(1, tensors):
                q = lax.rem(x + j, tensors)
                igrad_t = dot_nn(ow[q].T, gt_ref[s]).astype(BF16)
                rhs[s, pl.ds(pl.multiple_of(k + q * kq, kq), kq)] = dot_nn(igrad_t, xs).astype(BF16)
                comp = dot_nn(pt[q], xs).astype(BF16)
                rhs[s, block(q)] = comp
                f_rhs[s, block(q)] = dot_nn(comp, xt).astype(BF16)
            lhs[i, :, :k] = dot_nn(gs, f_lhs[s, :, :k]).astype(BF16)
            grad = dot_nn(lhs[i], rhs[s]) + gs.astype(F32)
            own = grad[:, :dq]
            for q in range(1, tensors):
                own = jnp.where(x == q, grad[:, q * dq:(q + 1) * dq], own)
            eg[s] = own.reshape(tables, nr, dq).astype(BF16)
            lo[s] = (dot_nn(f_lhs[s], f_rhs[s]) + xt.astype(F32)).astype(BF16)
        for j in range(1, tables):
            e_copy(c, j).start()
        e_store(c).start()
        lo_store(c).start()
        reduce_step(c)
        return carry

    lax.fori_loop(0, chunks, second, 0)

    if fused:
        for j in range(1, tables):
            ag_table(j).wait_recv()
        grads[0][...] = fs[...]
    else:
        for ref, (acc, rows, scale) in zip(grads, layout):
            ref[...] = acc[:, :ref.shape[1]] * scale

    for c in range(chunks):
        lo_store(c).wait()
        e_store(c).wait()
        for j in range(1, tables):
            e_copy(c, j).wait_recv()
    for c in range(chunks):
        for j in range(1, tables):
            x_copy(c, j).wait_send()
            e_copy(c, j).wait_send()
    for j in range(1, tensors):
        for i in range(3):
            w_copy(i, j).wait_send()
    if fused:
        for j in range(1, tables):
            rs_table(j).wait_send()
            ag_table(j).wait_send()
        for j in range(1, reps):
            rs_rep(j).wait_send()
            ag_rep(j).wait_send()


def write_kernel(layer, emb, pieces, layer_out, emb_out, lc_g, proj_g, out_g, sems):
    copies = [
        pltpu.make_async_copy(src, dst, sems.at[i])
        for i, (src, dst) in enumerate(((layer, layer_out), (emb, emb_out)))
    ]
    for copy in copies:
        copy.start()
    at = 0
    wide = []
    for rows in (lc_g.shape[0], proj_g.shape[1], out_g.shape[1]):
        halves = []
        for _ in range(lc_g.shape[1] // 128):
            halves.append(pieces[at:at + rows // 16].reshape(rows, 128).astype(F32))
            at += rows // 16
        wide.append(halves)
    lc_g[...] = jnp.concatenate(wide[0], axis=1)
    proj_g[...] = jnp.concatenate([half.T for half in wide[1]], axis=0)
    out_g[...] = jnp.concatenate([half.T for half in wide[2]], axis=0)[:out_g.shape[0]]
    for copy in copies:
        copy.wait()


def shards(sizes, pooled, lc_weight, fm_proj, fm_out, cotangent):
    tables, reps, tensors = sizes["table"], sizes["rep"], sizes["tensor"]
    samples, n, d = cotangent.shape
    nr = pooled.shape[1]
    jq, kq, dq = lc_weight.shape[0], fm_out.shape[0], d // tensors
    total = samples * reps * tables
    cs = 2 if samples % 2 == 0 else 1
    chunks = samples // cs
    wide = -(-d // 128) * 128
    pieces = (n // 128) * (jq // 16 + kq // 16) + (wide // 128) * (kq // 16)
    group = tables * reps
    fused = pieces % group == 0 and wide == n and jq % 16 == 0 and kq % 16 == 0
    pp = pieces // group if fused else 1
    cfg = dict(
        tables=tables, reps=reps, tensors=tensors, samples=samples, nr=nr, n=n, d=d, kq=kq, jq=jq, dq=dq,
        cs=cs, pp=pp, fused=fused,
        wide_scale=float(total * d) ** (-0.5), out_scale=float(total * n * d) ** (-0.5),
    )
    part = reps * pp if fused else 1
    held = pieces if fused else 1
    dma = pltpu.SemaphoreType.DMA
    peers = max(tables - 1, 1)
    wpeers = max(tensors - 1, 1)
    rpeers = max(tables - 1, reps - 1, 1)
    k = kq * tensors
    scratch = [
        pltpu.VMEM((samples, tables, nr, d), BF16),
        pltpu.VMEM((samples, d, n), BF16),
        pltpu.VMEM((tensors, n, kq), BF16),
        pltpu.VMEM((tensors, jq, n), BF16),
        pltpu.VMEM((tensors, d, kq), BF16),
        pltpu.VMEM((tensors, kq, n), BF16),
        pltpu.VMEM((cs, n, 2 * k + n), BF16),
        pltpu.VMEM((samples, 2 * k + n, d), BF16),
        pltpu.VMEM((samples, d, k + n), BF16),
        pltpu.VMEM((samples, k + n, n), BF16),
        pltpu.VMEM((samples, kq, n), BF16),
        pltpu.VMEM((samples, d, n), BF16),
        pltpu.VMEM((samples, tables, nr, dq), BF16),
        pltpu.VMEM((jq, n), F32),
        pltpu.VMEM((kq, n), F32),
        pltpu.VMEM((kq, wide), F32),
        pltpu.VMEM((held, 16, 128), BF16),
        pltpu.VMEM((peers, part, 16, 128), BF16),
        pltpu.VMEM((part, 16, 128), BF16),
        pltpu.VMEM((max(reps - 1, 1), pp, 16, 128), BF16),
        pltpu.VMEM((held, 16, 128), BF16),
        dma((3 * chunks + 4,)),
        dma((chunks, peers)),
        dma((chunks, peers)),
        dma((3, wpeers)),
        dma((3, wpeers)),
        dma((chunks, peers)),
        dma((chunks, peers)),
        dma((4, rpeers)),
        dma((4, rpeers)),
    ]
    hbm = pl.BlockSpec(memory_space=pl.ANY)
    vmem = pl.BlockSpec(memory_space=pltpu.VMEM)
    layer_shape = jax.ShapeDtypeStruct((samples, d, n), BF16)
    emb_shape = jax.ShapeDtypeStruct((pooled.shape[0], nr, dq), BF16)
    if fused:
        grad_shapes = (jax.ShapeDtypeStruct((pieces, 16, 128), BF16),)
    else:
        grad_shapes = tuple(jax.ShapeDtypeStruct(s, F32) for s in ((jq, n), (kq, n), (kq, d)))
    layer, emb, *grads = pl.pallas_call(
        functools.partial(layer_kernel, cfg),
        out_shape=(layer_shape, emb_shape, *grad_shapes),
        in_specs=[hbm] * 5,
        out_specs=(hbm, hbm) + (vmem,) * len(grad_shapes),
        scratch_shapes=scratch,
        compiler_params=pltpu.CompilerParams(
            collective_id=0, has_side_effects=True, vmem_limit_bytes=VMEM_BYTES
        ),
        name="interaction_layer",
    )(pooled, lc_weight, fm_proj, fm_out.T, cotangent.transpose(0, 2, 1))
    if fused:
        layer, emb, lc_g, proj_g, out_t = pl.pallas_call(
            write_kernel,
            out_shape=(
                layer_shape,
                emb_shape,
                jax.ShapeDtypeStruct((jq, n), F32),
                jax.ShapeDtypeStruct((n, kq), F32),
                jax.ShapeDtypeStruct((d, kq), F32),
            ),
            in_specs=[hbm, hbm, vmem],
            out_specs=(hbm, hbm, vmem, vmem, vmem),
            scratch_shapes=[dma((2,))],
            compiler_params=pltpu.CompilerParams(vmem_limit_bytes=VMEM_BYTES),
            name="write_outputs",
        )(layer, emb, *grads)
        out_g = out_t.T
    else:
        lc_g, proj_t, out_g = lax.psum(tuple(grads), ("rep", "table"))
        proj_g = proj_t.T
    return layer.transpose(0, 2, 1), emb, lc_g, proj_g, out_g


def solution(mesh):
    in_specs = (
        P("rep", "table", None),
        P("tensor", None),
        P(None, "tensor"),
        P("tensor", None),
        P(("rep", "table"), None, None),
    )
    out_specs = (
        P(("rep", "table"), None, None),
        P("rep", "table", "tensor"),
        P("tensor", None),
        P(None, "tensor"),
        P("tensor", None),
    )
    return jax.shard_map(
        functools.partial(shards, dict(mesh.shape)),
        mesh=mesh, in_specs=in_specs, out_specs=out_specs, check_vma=False,
    )
```

```python
import functools

import jax
import jax.numpy as jnp
from jax import lax
from jax.experimental import pallas as pl
from jax.experimental.pallas import tpu as pltpu
from jax.sharding import PartitionSpec as P

MESH = pl.DeviceIdType.MESH
BF16 = jnp.bfloat16
F32 = jnp.float32
VMEM_BYTES = 60 * 1024 * 1024


def dot_nn(a, b):
    return jnp.dot(a, b, preferred_element_type=F32)


def layer_kernel(cfg, pooled, lc_w, proj_w, out_w, cot, layer, emb, *rest):
    tables, reps, tensors = cfg["tables"], cfg["reps"], cfg["tensors"]
    samples, nr, n, d = cfg["samples"], cfg["nr"], cfg["n"], cfg["d"]
    kq, jq, dq, cs, pp, fused = cfg["kq"], cfg["jq"], cfg["dq"], cfg["cs"], cfg["pp"], cfg["fused"]
    grads, scratch = (rest[:1], rest[1:]) if fused else (rest[:3], rest[3:])
    (x_ref, gt_ref, g_ref, xt_ref, pw, ww, ow, p_rel, ot_rel, own_ct, own_cgt, own_it, igt, lo, eg, acc_l, acc_p, acc_o,
     gb, rb1, sb, rb2, fs, loc, x_send, x_recv, w_send, w_recv, e_send, e_recv, r_send, r_recv) = scratch
    chunks = samples // cs
    t = lax.axis_index("table")
    r = lax.axis_index("rep")
    x = lax.axis_index("tensor")

    def peer(axis, me, size, j):
        return {axis: lax.rem(me + j, size)}

    barrier = pltpu.get_barrier_semaphore()
    groups = [("table", t, tables), ("tensor", x, tensors)] + ([("rep", r, reps)] if fused else [])
    signals = 0
    for axis, me, size in groups:
        for j in range(1, size):
            pl.semaphore_signal(barrier, inc=1, device_id=peer(axis, me, size, j), device_id_type=MESH)
            signals += 1

    g_load = pltpu.make_async_copy(cot, gt_ref, loc.at[chunks])

    def x_load(c):
        return pltpu.make_async_copy(
            pooled.at[pl.ds(t * samples + c * cs, cs)], x_ref.at[pl.ds(c * cs, cs), t], loc.at[c]
        )

    w_pairs = ((proj_w, pw), (out_w, ow), (lc_w, ww))
    w_loads = [
        pltpu.make_async_copy(src, dst.at[x], loc.at[chunks + 1 + i]) for i, (src, dst) in enumerate(w_pairs)
    ]
    for load in w_loads:
        load.start()
    g_load.start()
    for c in range(chunks):
        x_load(c).start()
    pl.semaphore_wait(barrier, signals)

    def x_copy(c, j):
        to = lax.rem(t + j, tables)
        return pltpu.make_async_remote_copy(
            pooled.at[pl.ds(to * samples + c * cs, cs)],
            x_ref.at[pl.ds(c * cs, cs), t],
            x_send.at[c, j - 1],
            x_recv.at[c, j - 1],
            device_id=peer("table", t, tables, j),
            device_id_type=MESH,
        )

    def w_copy(i, j):
        src, dst = w_pairs[i]
        return pltpu.make_async_remote_copy(
            src, dst.at[x], w_send.at[i, j - 1], w_recv.at[i, j - 1],
            device_id=peer("tensor", x, tensors, j), device_id_type=MESH,
        )

    for c in range(chunks):
        for j in range(1, tables):
            x_copy(c, j).start()
    for j in range(1, tensors):
        for i in range(3):
            w_copy(i, j).start()

    for load in w_loads:
        load.wait()
    own_pt, own_o = pw[x].T, ow[x].T
    acc_l[...] = jnp.zeros_like(acc_l)
    acc_p[...] = jnp.zeros_like(acc_p)
    acc_o[...] = jnp.zeros_like(acc_o)
    g_load.wait()

    def before(c, carry):
        at = [c * cs + i for i in range(cs)]
        for s in at:
            gt = gt_ref[s]
            g_ref[s] = gt.T
            igt[s] = dot_nn(own_o, gt).astype(BF16)
        return carry

    lax.fori_loop(0, chunks, before, 0)

    def first(c, carry):
        x_load(c).wait()
        for j in range(1, tables):
            x_copy(c, j).wait_recv()
        at = [c * cs + i for i in range(cs)]
        own_rows = [x_ref[s, pl.ds(x * (jq // nr), jq // nr)].reshape(jq, d) for s in at]
        xs = [x_ref[s].reshape(n, d) for s in at]
        xt = [v.T for v in xs]
        comp = [dot_nn(own_pt, v).astype(BF16) for v in xs]
        cgrad = [dot_nn(igt[s], v).astype(BF16) for s, v in zip(at, xs)]
        sum_l = acc_l[...]
        for s, v in zip(at, own_rows):
            sum_l = sum_l + dot_nn(v, gt_ref[s])
        inter = [dot_nn(v, w).astype(BF16) for v, w in zip(comp, xt)]
        sum_p = acc_p[...]
        for v, w in zip(cgrad, xt):
            sum_p = sum_p + dot_nn(v, w)
        sum_o = acc_o[:, :d]
        for s, v in zip(at, inter):
            sum_o = sum_o + dot_nn(v, g_ref[s])
        acc_l[...] = sum_l
        acc_p[...] = sum_p
        acc_o[:, :d] = sum_o
        for i, s in enumerate(at):
            xt_ref[s] = xt[i]
            own_ct[s] = comp[i]
            own_cgt[s] = cgrad[i]
            own_it[s] = inter[i]
        return carry

    lax.fori_loop(0, chunks, first, 0)

    part = reps * pp

    def rs_table(j):
        to = lax.rem(t + j, tables)
        return pltpu.make_async_remote_copy(
            gb.at[pl.ds(to * part, part)], rb1.at[j - 1], r_send.at[0, j - 1], r_recv.at[0, j - 1],
            device_id=peer("table", t, tables, j), device_id_type=MESH,
        )

    def rs_rep(j):
        to = lax.rem(r + j, reps)
        return pltpu.make_async_remote_copy(
            sb.at[pl.ds(to * pp, pp)], rb2.at[j - 1], r_send.at[1, j - 1], r_recv.at[1, j - 1],
            device_id=peer("rep", r, reps, j), device_id_type=MESH,
        )

    def ag_rep(j):
        mine = fs.at[pl.ds(t * part + r * pp, pp)]
        return pltpu.make_async_remote_copy(
            mine, mine, r_send.at[2, j - 1], r_recv.at[2, j - 1],
            device_id=peer("rep", r, reps, j), device_id_type=MESH,
        )

    def ag_table(j):
        mine = fs.at[pl.ds(t * part, part)]
        return pltpu.make_async_remote_copy(
            mine, mine, r_send.at[3, j - 1], r_recv.at[3, j - 1],
            device_id=peer("table", t, tables, j), device_id_type=MESH,
        )

    layout = ((acc_l, jq, cfg["wide_scale"]), (acc_p, kq, cfg["wide_scale"]), (acc_o, kq, cfg["out_scale"]))
    if fused:
        at = 0
        for ref, rows, scale in layout:
            for h in range(n // 128):
                value = (ref[:, h * 128:(h + 1) * 128] * scale).astype(BF16)
                gb[at:at + rows // 16] = value.reshape(rows // 16, 16, 128)
                at += rows // 16
        for j in range(1, tables):
            rs_table(j).start()

    def reduce_step(c):
        if not fused:
            return

        @pl.when(c == 0)
        def _():
            total = gb[pl.ds(t * part, part)].astype(F32)
            for j in range(1, tables):
                rs_table(j).wait_recv()
                total = total + rb1[j - 1].astype(F32)
            sb[...] = total.astype(BF16)
            for j in range(1, reps):
                rs_rep(j).start()

        @pl.when(c == 1)
        def _():
            total = sb[pl.ds(r * pp, pp)].astype(F32)
            for j in range(1, reps):
                rs_rep(j).wait_recv()
                total = total + rb2[j - 1].astype(F32)
            fs[pl.ds(t * part + r * pp, pp)] = total.astype(BF16)
            for j in range(1, reps):
                ag_rep(j).start()

        @pl.when(c == 2)
        def _():
            for j in range(1, reps):
                ag_rep(j).wait_recv()
            for j in range(1, tables):
                ag_table(j).start()

    for j in range(1, tensors):
        for i in range(3):
            w_copy(i, j).wait_recv()
    order = [x] + [lax.rem(x + j, tensors) for j in range(1, tensors)]
    p_rel[...] = jnp.concatenate([pw[q] for q in order], axis=1)
    ot_rel[...] = jnp.concatenate([ow[q] for q in order], axis=1)
    other_pt = [pw[q].T for q in order[1:]]
    other_o = [ow[q].T for q in order[1:]]

    def lo_store(c):
        rows = pl.ds(c * cs, cs)
        return pltpu.make_async_copy(lo.at[rows], layer.at[rows], loc.at[chunks + 4 + c])

    def e_store(c):
        return pltpu.make_async_copy(
            eg.at[pl.ds(c * cs, cs), t], emb.at[pl.ds(t * samples + c * cs, cs)], loc.at[2 * chunks + 4 + c]
        )

    def e_copy(c, j):
        to = lax.rem(t + j, tables)
        return pltpu.make_async_remote_copy(
            eg.at[pl.ds(c * cs, cs), to],
            emb.at[pl.ds(t * samples + c * cs, cs)],
            e_send.at[c, j - 1],
            e_recv.at[c, j - 1],
            device_id=peer("table", t, tables, j),
            device_id_type=MESH,
        )

    def second(c, carry):
        at = [c * cs + i for i in range(cs)]
        xs = [x_ref[s].reshape(n, d) for s in at]
        w_all = ww[...].reshape(n, n)
        igrad_t = [[dot_nn(v, gt_ref[s]).astype(BF16) for v in other_o] for s in at]
        comp = [[dot_nn(v, w).astype(BF16) for v in other_pt] for w in xs]
        igrad = [dot_nn(g_ref[s], ot_rel[...]).astype(BF16) for s in at]
        cgrad = [[dot_nn(v, w).astype(BF16) for v in vs] for vs, w in zip(igrad_t, xs)]
        inter = [[dot_nn(v, xt_ref[s]).astype(BF16) for v in vs] for vs, s in zip(comp, at)]
        for i, s in enumerate(at):
            gs = g_ref[s]
            left = jnp.concatenate([igrad[i], p_rel[...], w_all], axis=1)
            right = jnp.concatenate([own_ct[s], *comp[i], own_cgt[s], *cgrad[i], gs], axis=0)
            grad = dot_nn(left, right) + gs.astype(F32)
            own = grad[:, :dq]
            for q in range(1, tensors):
                own = jnp.where(x == q, grad[:, q * dq:(q + 1) * dq], own)
            eg[s] = own.reshape(tables, nr, dq).astype(BF16)
        for j in range(1, tables):
            e_copy(c, j).start()
        e_store(c).start()
        for i, s in enumerate(at):
            xt = xt_ref[s]
            left = jnp.concatenate([ot_rel[...], xt], axis=1)
            right = jnp.concatenate([own_it[s], *inter[i], w_all], axis=0)
            lo[s] = (dot_nn(left, right) + xt.astype(F32)).astype(BF16)
        lo_store(c).start()
        reduce_step(c)
        return carry

    lax.fori_loop(0, chunks, second, 0)

    if fused:
        for j in range(1, tables):
            ag_table(j).wait_recv()
        grads[0][...] = fs[...]
    else:
        for ref, (acc, rows, scale) in zip(grads, layout):
            ref[...] = acc[:, :ref.shape[1]] * scale

    for c in range(chunks):
        lo_store(c).wait()
        e_store(c).wait()
        for j in range(1, tables):
            e_copy(c, j).wait_recv()
    for c in range(chunks):
        for j in range(1, tables):
            x_copy(c, j).wait_send()
            e_copy(c, j).wait_send()
    for j in range(1, tensors):
        for i in range(3):
            w_copy(i, j).wait_send()
    if fused:
        for j in range(1, tables):
            rs_table(j).wait_send()
            ag_table(j).wait_send()
        for j in range(1, reps):
            rs_rep(j).wait_send()
            ag_rep(j).wait_send()


def write_kernel(layer, emb, pieces, layer_out, emb_out, lc_g, proj_g, out_g, held_l, held_e, sems):
    loads, stores = [], []
    for src, held, dst in ((layer, held_l, layer_out), (emb, held_e, emb_out)):
        parts = 4 if src.shape[0] % 4 == 0 else 1
        size = src.shape[0] // parts
        for p in range(parts):
            rows = pl.ds(p * size, size)
            at = len(loads)
            loads.append(pltpu.make_async_copy(src.at[rows], held.at[rows], sems.at[0, at]))
            stores.append(pltpu.make_async_copy(held.at[rows], dst.at[rows], sems.at[1, at]))
    for load in loads:
        load.start()
    for load, store in zip(loads, stores):
        load.wait()
        store.start()
    at = 0
    wide = []
    for rows in (lc_g.shape[0], proj_g.shape[1], out_g.shape[1]):
        halves = []
        for _ in range(lc_g.shape[1] // 128):
            halves.append(pieces[at:at + rows // 16].reshape(rows, 128).astype(F32))
            at += rows // 16
        wide.append(halves)
    lc_g[...] = jnp.concatenate(wide[0], axis=1)
    proj_g[...] = jnp.concatenate([half.T for half in wide[1]], axis=0)
    out_g[...] = jnp.concatenate([half.T for half in wide[2]], axis=0)[:out_g.shape[0]]
    for store in stores:
        store.wait()


def shards(sizes, pooled, lc_weight, fm_proj, fm_out, cotangent):
    tables, reps, tensors = sizes["table"], sizes["rep"], sizes["tensor"]
    samples, n, d = cotangent.shape
    nr = pooled.shape[1]
    jq, kq, dq = lc_weight.shape[0], fm_out.shape[0], d // tensors
    total = samples * reps * tables
    cs = 2 if samples % 2 == 0 else 1
    chunks = samples // cs
    wide = -(-d // 128) * 128
    pieces = (n // 128) * (jq // 16 + kq // 16) + (wide // 128) * (kq // 16)
    group = tables * reps
    fused = pieces % group == 0 and wide == n and jq % 16 == 0 and kq % 16 == 0
    pp = pieces // group if fused else 1
    cfg = dict(
        tables=tables, reps=reps, tensors=tensors, samples=samples, nr=nr, n=n, d=d, kq=kq, jq=jq, dq=dq,
        cs=cs, pp=pp, fused=fused,
        wide_scale=float(total * d) ** (-0.5), out_scale=float(total * n * d) ** (-0.5),
    )
    part = reps * pp if fused else 1
    held = pieces if fused else 1
    dma = pltpu.SemaphoreType.DMA
    peers = max(tables - 1, 1)
    wpeers = max(tensors - 1, 1)
    rpeers = max(tables - 1, reps - 1, 1)
    k = kq * tensors
    scratch = [
        pltpu.VMEM((samples, tables, nr, d), BF16),
        pltpu.VMEM((samples, d, n), BF16),
        pltpu.VMEM((samples, n, d), BF16),
        pltpu.VMEM((samples, d, n), BF16),
        pltpu.VMEM((tensors, n, kq), BF16),
        pltpu.VMEM((tensors, jq, n), BF16),
        pltpu.VMEM((tensors, d, kq), BF16),
        pltpu.VMEM((n, k), BF16),
        pltpu.VMEM((d, k), BF16),
        pltpu.VMEM((samples, kq, d), BF16),
        pltpu.VMEM((samples, kq, d), BF16),
        pltpu.VMEM((samples, kq, n), BF16),
        pltpu.VMEM((samples, kq, n), BF16),
        pltpu.VMEM((samples, d, n), BF16),
        pltpu.VMEM((samples, tables, nr, dq), BF16),
        pltpu.VMEM((jq, n), F32),
        pltpu.VMEM((kq, n), F32),
        pltpu.VMEM((kq, wide), F32),
        pltpu.VMEM((held, 16, 128), BF16),
        pltpu.VMEM((peers, part, 16, 128), BF16),
        pltpu.VMEM((part, 16, 128), BF16),
        pltpu.VMEM((max(reps - 1, 1), pp, 16, 128), BF16),
        pltpu.VMEM((held, 16, 128), BF16),
        dma((3 * chunks + 4,)),
        dma((chunks, peers)),
        dma((chunks, peers)),
        dma((3, wpeers)),
        dma((3, wpeers)),
        dma((chunks, peers)),
        dma((chunks, peers)),
        dma((4, rpeers)),
        dma((4, rpeers)),
    ]
    hbm = pl.BlockSpec(memory_space=pl.ANY)
    vmem = pl.BlockSpec(memory_space=pltpu.VMEM)
    layer_shape = jax.ShapeDtypeStruct((samples, d, n), BF16)
    emb_shape = jax.ShapeDtypeStruct((pooled.shape[0], nr, dq), BF16)
    if fused:
        grad_shapes = (jax.ShapeDtypeStruct((pieces, 16, 128), BF16),)
    else:
        grad_shapes = tuple(jax.ShapeDtypeStruct(s, F32) for s in ((jq, n), (kq, n), (kq, d)))
    layer, emb, *grads = pl.pallas_call(
        functools.partial(layer_kernel, cfg),
        out_shape=(layer_shape, emb_shape, *grad_shapes),
        in_specs=[hbm] * 5,
        out_specs=(hbm, hbm) + (vmem,) * len(grad_shapes),
        scratch_shapes=scratch,
        compiler_params=pltpu.CompilerParams(
            collective_id=0, has_side_effects=True, vmem_limit_bytes=VMEM_BYTES
        ),
        name="interaction_layer",
    )(pooled, lc_weight, fm_proj, fm_out.T, cotangent.transpose(0, 2, 1))
    if fused:
        layer, emb, lc_g, proj_g, out_t = pl.pallas_call(
            write_kernel,
            out_shape=(
                layer_shape,
                emb_shape,
                jax.ShapeDtypeStruct((jq, n), F32),
                jax.ShapeDtypeStruct((n, kq), F32),
                jax.ShapeDtypeStruct((d, kq), F32),
            ),
            in_specs=[hbm, hbm, vmem],
            out_specs=(hbm, hbm, vmem, vmem, vmem),
            scratch_shapes=[
                pltpu.VMEM(layer_shape.shape, BF16), pltpu.VMEM(emb_shape.shape, BF16), dma((2, 8)),
            ],
            compiler_params=pltpu.CompilerParams(vmem_limit_bytes=VMEM_BYTES),
            name="write_outputs",
        )(layer, emb, *grads)
        out_g = out_t.T
    else:
        lc_g, proj_t, out_g = lax.psum(tuple(grads), ("rep", "table"))
        proj_g = proj_t.T
    return layer.transpose(0, 2, 1), emb, lc_g, proj_g, out_g


def solution(mesh):
    in_specs = (
        P("rep", "table", None),
        P("tensor", None),
        P(None, "tensor"),
        P("tensor", None),
        P(("rep", "table"), None, None),
    )
    out_specs = (
        P(("rep", "table"), None, None),
        P("rep", "table", "tensor"),
        P("tensor", None),
        P(None, "tensor"),
        P("tensor", None),
    )
    return jax.shard_map(
        functools.partial(shards, dict(mesh.shape)),
        mesh=mesh, in_specs=in_specs, out_specs=out_specs, check_vma=False,
    )
```

```python
import functools

import jax
import jax.numpy as jnp
from jax import lax
from jax.experimental import pallas as pl
from jax.experimental.pallas import tpu as pltpu
from jax.sharding import PartitionSpec as P

MESH = pl.DeviceIdType.MESH
BF16 = jnp.bfloat16
F32 = jnp.float32
VMEM_BYTES = 60 * 1024 * 1024


def dot_nn(a, b):
    return jnp.dot(a, b, preferred_element_type=F32)


def layer_kernel(cfg, pooled, lc_w, proj_w, out_w, cot, layer, emb, *rest):
    tables, reps, tensors = cfg["tables"], cfg["reps"], cfg["tensors"]
    samples, nr, n, d = cfg["samples"], cfg["nr"], cfg["n"], cfg["d"]
    kq, jq, dq, cs, pp, fused = cfg["kq"], cfg["jq"], cfg["dq"], cfg["cs"], cfg["pp"], cfg["fused"]
    grads, scratch = (rest[:1], rest[1:]) if fused else (rest[:3], rest[3:])
    (x_ref, gt_ref, g_ref, xt_ref, pw, ww, ow, p_rel, ot_rel, own_ct, own_cgt, own_it, igt, lo, eg, acc_l, acc_p, acc_o,
     gb, rb1, sb, rb2, fs, loc, x_send, x_recv, w_send, w_recv, f_send, f_recv, c_send, c_recv, e_send, e_recv, r_send, r_recv) = scratch
    chunks = samples // cs
    t = lax.axis_index("table")
    r = lax.axis_index("rep")
    x = lax.axis_index("tensor")

    def peer(axis, me, size, j):
        return {axis: lax.rem(me + j, size)}

    barrier = pltpu.get_barrier_semaphore()
    groups = [("table", t, tables), ("tensor", x, tensors)] + ([("rep", r, reps)] if fused else [])
    signals = 0
    for axis, me, size in groups:
        for j in range(1, size):
            pl.semaphore_signal(barrier, inc=1, device_id=peer(axis, me, size, j), device_id_type=MESH)
            signals += 1

    g_load = pltpu.make_async_copy(cot, gt_ref, loc.at[chunks])

    def x_load(c):
        return pltpu.make_async_copy(
            pooled.at[pl.ds(t * samples + c * cs, cs)], x_ref.at[pl.ds(c * cs, cs), t], loc.at[c]
        )

    w_pairs = ((proj_w, pw), (out_w, ow), (lc_w, ww))
    w_loads = [
        pltpu.make_async_copy(src, dst.at[x], loc.at[chunks + 1 + i]) for i, (src, dst) in enumerate(w_pairs)
    ]
    for load in w_loads:
        load.start()
    g_load.start()
    for c in range(chunks):
        x_load(c).start()
    pl.semaphore_wait(barrier, signals)

    chips, rounds = tables // 2, chunks // tensors
    chip, core = t // 2, lax.rem(t, 2)
    mate = chip * 2 + lax.rem(core + 1, 2)

    def c_copy(c):
        return pltpu.make_async_remote_copy(
            pooled.at[pl.ds(mate * samples + c * cs, cs)],
            x_ref.at[pl.ds(c * cs, cs), t],
            c_send.at[c],
            c_recv.at[c],
            device_id={"table": mate},
            device_id_type=MESH,
        )

    def x_copy(g, a, b):
        to = lax.rem(chip + a, chips) * 2 + lax.rem(core + b, 2)
        first_row = (g * tensors + x) * cs
        return pltpu.make_async_remote_copy(
            pooled.at[pl.ds(to * samples + first_row, cs)],
            x_ref.at[pl.ds(first_row, cs), t],
            x_send.at[g, a - 1, b],
            x_recv.at[g, a - 1, b],
            device_id={"table": to},
            device_id_type=MESH,
        )

    def f_copy(g, a, j):
        source = lax.rem(chip + chips - a, chips) * 2
        held = x_ref.at[pl.ds((g * tensors + x) * cs, cs), pl.ds(source, 2)]
        return pltpu.make_async_remote_copy(
            held, held, f_send.at[g, a - 1, j - 1], f_recv.at[g, a - 1, j - 1],
            device_id=peer("tensor", x, tensors, j), device_id_type=MESH,
        )

    def pass_on(g):
        for a in range(1, chips):
            for b in range(2):
                x_copy(g, a, b).wait_recv()
            for j in range(1, tensors):
                f_copy(g, a, j).start()

    def w_copy(i, j):
        src, dst = w_pairs[i]
        return pltpu.make_async_remote_copy(
            src, dst.at[x], w_send.at[i, j - 1], w_recv.at[i, j - 1],
            device_id=peer("tensor", x, tensors, j), device_id_type=MESH,
        )

    for g in range(rounds):
        for a in range(1, chips):
            for b in range(2):
                x_copy(g, a, b).start()
    for c in range(chunks):
        c_copy(c).start()
    for j in range(1, tensors):
        for i in range(3):
            w_copy(i, j).start()

    for load in w_loads:
        load.wait()
    own_pt, own_o = pw[x].T, ow[x].T
    acc_l[...] = jnp.zeros_like(acc_l)
    acc_p[...] = jnp.zeros_like(acc_p)
    acc_o[...] = jnp.zeros_like(acc_o)
    g_load.wait()

    def before(c, carry):
        at = [c * cs + i for i in range(cs)]
        for s in at:
            gt = gt_ref[s]
            g_ref[s] = gt.T
            igt[s] = dot_nn(own_o, gt).astype(BF16)
        return carry

    lax.fori_loop(0, chunks, before, 0)

    def first(c):
        at = [c * cs + i for i in range(cs)]
        own_rows = [x_ref[s, pl.ds(x * (jq // nr), jq // nr)].reshape(jq, d) for s in at]
        xs = [x_ref[s].reshape(n, d) for s in at]
        xt = [v.T for v in xs]
        comp = [dot_nn(own_pt, v).astype(BF16) for v in xs]
        cgrad = [dot_nn(igt[s], v).astype(BF16) for s, v in zip(at, xs)]
        sum_l = acc_l[...]
        for s, v in zip(at, own_rows):
            sum_l = sum_l + dot_nn(v, gt_ref[s])
        inter = [dot_nn(v, w).astype(BF16) for v, w in zip(comp, xt)]
        sum_p = acc_p[...]
        for v, w in zip(cgrad, xt):
            sum_p = sum_p + dot_nn(v, w)
        sum_o = acc_o[:, :d]
        for s, v in zip(at, inter):
            sum_o = sum_o + dot_nn(v, g_ref[s])
        acc_l[...] = sum_l
        acc_p[...] = sum_p
        acc_o[:, :d] = sum_o
        for i, s in enumerate(at):
            xt_ref[s] = xt[i]
            own_ct[s] = comp[i]
            own_cgt[s] = cgrad[i]
            own_it[s] = inter[i]

    for c in range(chunks):
        x_load(c).wait()
        c_copy(c).wait_recv()
    pass_on(0)
    for g in range(rounds):
        first(g * tensors + x)
        if g + 1 < rounds:
            pass_on(g + 1)
        for j in range(1, tensors):
            for a in range(1, chips):
                f_copy(g, a, j).wait_recv()
            first(g * tensors + lax.rem(x + tensors - j, tensors))

    part = reps * pp

    def rs_table(j):
        to = lax.rem(t + j, tables)
        return pltpu.make_async_remote_copy(
            gb.at[pl.ds(to * part, part)], rb1.at[j - 1], r_send.at[0, j - 1], r_recv.at[0, j - 1],
            device_id=peer("table", t, tables, j), device_id_type=MESH,
        )

    def rs_rep(j):
        to = lax.rem(r + j, reps)
        return pltpu.make_async_remote_copy(
            sb.at[pl.ds(to * pp, pp)], rb2.at[j - 1], r_send.at[1, j - 1], r_recv.at[1, j - 1],
            device_id=peer("rep", r, reps, j), device_id_type=MESH,
        )

    def ag_rep(j):
        mine = fs.at[pl.ds(t * part + r * pp, pp)]
        return pltpu.make_async_remote_copy(
            mine, mine, r_send.at[2, j - 1], r_recv.at[2, j - 1],
            device_id=peer("rep", r, reps, j), device_id_type=MESH,
        )

    def ag_table(j):
        mine = fs.at[pl.ds(t * part, part)]
        return pltpu.make_async_remote_copy(
            mine, mine, r_send.at[3, j - 1], r_recv.at[3, j - 1],
            device_id=peer("table", t, tables, j), device_id_type=MESH,
        )

    layout = ((acc_l, jq, cfg["wide_scale"]), (acc_p, kq, cfg["wide_scale"]), (acc_o, kq, cfg["out_scale"]))
    if fused:
        at = 0
        for ref, rows, scale in layout:
            for h in range(n // 128):
                value = (ref[:, h * 128:(h + 1) * 128] * scale).astype(BF16)
                gb[at:at + rows // 16] = value.reshape(rows // 16, 16, 128)
                at += rows // 16
        for j in range(1, tables):
            rs_table(j).start()

    def reduce_step(c):
        if not fused:
            return

        @pl.when(c == 0)
        def _():
            total = gb[pl.ds(t * part, part)].astype(F32)
            for j in range(1, tables):
                rs_table(j).wait_recv()
                total = total + rb1[j - 1].astype(F32)
            sb[...] = total.astype(BF16)
            for j in range(1, reps):
                rs_rep(j).start()

        @pl.when(c == 1)
        def _():
            total = sb[pl.ds(r * pp, pp)].astype(F32)
            for j in range(1, reps):
                rs_rep(j).wait_recv()
                total = total + rb2[j - 1].astype(F32)
            fs[pl.ds(t * part + r * pp, pp)] = total.astype(BF16)
            for j in range(1, reps):
                ag_rep(j).start()

        @pl.when(c == 2)
        def _():
            for j in range(1, reps):
                ag_rep(j).wait_recv()
            for j in range(1, tables):
                ag_table(j).start()

    for j in range(1, tensors):
        for i in range(3):
            w_copy(i, j).wait_recv()
    order = [x] + [lax.rem(x + j, tensors) for j in range(1, tensors)]
    p_rel[...] = jnp.concatenate([pw[q] for q in order], axis=1)
    ot_rel[...] = jnp.concatenate([ow[q] for q in order], axis=1)
    other_pt = [pw[q].T for q in order[1:]]
    other_o = [ow[q].T for q in order[1:]]

    def lo_store(c):
        rows = pl.ds(c * cs, cs)
        return pltpu.make_async_copy(lo.at[rows], layer.at[rows], loc.at[chunks + 4 + c])

    def e_store(c):
        return pltpu.make_async_copy(
            eg.at[pl.ds(c * cs, cs), t], emb.at[pl.ds(t * samples + c * cs, cs)], loc.at[2 * chunks + 4 + c]
        )

    def e_copy(c, j):
        to = lax.rem(t + j, tables)
        return pltpu.make_async_remote_copy(
            eg.at[pl.ds(c * cs, cs), to],
            emb.at[pl.ds(t * samples + c * cs, cs)],
            e_send.at[c, j - 1],
            e_recv.at[c, j - 1],
            device_id=peer("table", t, tables, j),
            device_id_type=MESH,
        )

    def second(c, carry):
        at = [c * cs + i for i in range(cs)]
        xs = [x_ref[s].reshape(n, d) for s in at]
        w_all = ww[...].reshape(n, n)
        igrad_t = [[dot_nn(v, gt_ref[s]).astype(BF16) for v in other_o] for s in at]
        comp = [[dot_nn(v, w).astype(BF16) for v in other_pt] for w in xs]
        igrad = [dot_nn(g_ref[s], ot_rel[...]).astype(BF16) for s in at]
        cgrad = [[dot_nn(v, w).astype(BF16) for v in vs] for vs, w in zip(igrad_t, xs)]
        inter = [[dot_nn(v, xt_ref[s]).astype(BF16) for v in vs] for vs, s in zip(comp, at)]
        for i, s in enumerate(at):
            gs = g_ref[s]
            left = jnp.concatenate([igrad[i], p_rel[...], w_all], axis=1)
            right = jnp.concatenate([own_ct[s], *comp[i], own_cgt[s], *cgrad[i], gs], axis=0)
            grad = dot_nn(left, right) + gs.astype(F32)
            own = grad[:, :dq]
            for q in range(1, tensors):
                own = jnp.where(x == q, grad[:, q * dq:(q + 1) * dq], own)
            eg[s] = own.reshape(tables, nr, dq).astype(BF16)
        for j in range(1, tables):
            e_copy(c, j).start()
        e_store(c).start()
        for i, s in enumerate(at):
            xt = xt_ref[s]
            left = jnp.concatenate([ot_rel[...], xt], axis=1)
            right = jnp.concatenate([own_it[s], *inter[i], w_all], axis=0)
            lo[s] = (dot_nn(left, right) + xt.astype(F32)).astype(BF16)
        lo_store(c).start()
        reduce_step(c)
        return carry

    lax.fori_loop(0, chunks, second, 0)

    if fused:
        for j in range(1, tables):
            ag_table(j).wait_recv()
        grads[0][...] = fs[...]
    else:
        for ref, (acc, rows, scale) in zip(grads, layout):
            ref[...] = acc[:, :ref.shape[1]] * scale

    for c in range(chunks):
        lo_store(c).wait()
        e_store(c).wait()
        for j in range(1, tables):
            e_copy(c, j).wait_recv()
    for c in range(chunks):
        c_copy(c).wait_send()
        for j in range(1, tables):
            e_copy(c, j).wait_send()
    for g in range(rounds):
        for a in range(1, chips):
            for b in range(2):
                x_copy(g, a, b).wait_send()
            for j in range(1, tensors):
                f_copy(g, a, j).wait_send()
    for j in range(1, tensors):
        for i in range(3):
            w_copy(i, j).wait_send()
    if fused:
        for j in range(1, tables):
            rs_table(j).wait_send()
            ag_table(j).wait_send()
        for j in range(1, reps):
            rs_rep(j).wait_send()
            ag_rep(j).wait_send()


def write_kernel(layer, emb, pieces, layer_out, emb_out, lc_g, proj_g, out_g,
                 held_l, held_e, held_g, lc_v, proj_v, out_v, sems):
    g_load = pltpu.make_async_copy(pieces, held_g, sems.at[0, 8])
    g_load.start()
    loads, stores = [], []
    for src, held, dst in ((layer, held_l, layer_out), (emb, held_e, emb_out)):
        parts = 4 if src.shape[0] % 4 == 0 else 1
        size = src.shape[0] // parts
        for p in range(parts):
            rows = pl.ds(p * size, size)
            at = len(loads)
            loads.append(pltpu.make_async_copy(src.at[rows], held.at[rows], sems.at[0, at]))
            stores.append(pltpu.make_async_copy(held.at[rows], dst.at[rows], sems.at[1, at]))
    for load in loads:
        load.start()
    g_load.wait()
    at = 0
    wide = []
    for rows in (lc_g.shape[0], proj_g.shape[1], out_g.shape[1]):
        halves = []
        for _ in range(lc_g.shape[1] // 128):
            halves.append(held_g[at:at + rows // 16].reshape(rows, 128).astype(F32))
            at += rows // 16
        wide.append(halves)
    lc_v[...] = jnp.concatenate(wide[0], axis=1)
    proj_v[...] = jnp.concatenate([half.T for half in wide[1]], axis=0)
    out_v[...] = jnp.concatenate([half.T for half in wide[2]], axis=0)[:out_g.shape[0]]
    for i, (held, dst) in enumerate(((lc_v, lc_g), (proj_v, proj_g), (out_v, out_g))):
        stores.append(pltpu.make_async_copy(held, dst, sems.at[1, 8 + i]))
        stores[-1].start()
    for load, store in zip(loads, stores):
        load.wait()
        store.start()
    for store in stores:
        store.wait()


def shards(sizes, pooled, lc_weight, fm_proj, fm_out, cotangent):
    tables, reps, tensors = sizes["table"], sizes["rep"], sizes["tensor"]
    samples, n, d = cotangent.shape
    nr = pooled.shape[1]
    jq, kq, dq = lc_weight.shape[0], fm_out.shape[0], d // tensors
    total = samples * reps * tables
    cs = 2 if samples % (2 * tensors) == 0 else 1
    chunks = samples // cs
    rounds, chips = chunks // tensors, tables // 2
    wide = -(-d // 128) * 128
    pieces = (n // 128) * (jq // 16 + kq // 16) + (wide // 128) * (kq // 16)
    group = tables * reps
    fused = pieces % group == 0 and wide == n and jq % 16 == 0 and kq % 16 == 0
    pp = pieces // group if fused else 1
    cfg = dict(
        tables=tables, reps=reps, tensors=tensors, samples=samples, nr=nr, n=n, d=d, kq=kq, jq=jq, dq=dq,
        cs=cs, pp=pp, fused=fused,
        wide_scale=float(total * d) ** (-0.5), out_scale=float(total * n * d) ** (-0.5),
    )
    part = reps * pp if fused else 1
    held = pieces if fused else 1
    dma = pltpu.SemaphoreType.DMA
    peers = max(tables - 1, 1)
    wpeers = max(tensors - 1, 1)
    rpeers = max(tables - 1, reps - 1, 1)
    k = kq * tensors
    scratch = [
        pltpu.VMEM((samples, tables, nr, d), BF16),
        pltpu.VMEM((samples, d, n), BF16),
        pltpu.VMEM((samples, n, d), BF16),
        pltpu.VMEM((samples, d, n), BF16),
        pltpu.VMEM((tensors, n, kq), BF16),
        pltpu.VMEM((tensors, jq, n), BF16),
        pltpu.VMEM((tensors, d, kq), BF16),
        pltpu.VMEM((n, k), BF16),
        pltpu.VMEM((d, k), BF16),
        pltpu.VMEM((samples, kq, d), BF16),
        pltpu.VMEM((samples, kq, d), BF16),
        pltpu.VMEM((samples, kq, n), BF16),
        pltpu.VMEM((samples, kq, n), BF16),
        pltpu.VMEM((samples, d, n), BF16),
        pltpu.VMEM((samples, tables, nr, dq), BF16),
        pltpu.VMEM((jq, n), F32),
        pltpu.VMEM((kq, n), F32),
        pltpu.VMEM((kq, wide), F32),
        pltpu.VMEM((held, 16, 128), BF16),
        pltpu.VMEM((peers, part, 16, 128), BF16),
        pltpu.VMEM((part, 16, 128), BF16),
        pltpu.VMEM((max(reps - 1, 1), pp, 16, 128), BF16),
        pltpu.VMEM((held, 16, 128), BF16),
        dma((3 * chunks + 4,)),
        dma((rounds, max(chips - 1, 1), 2)),
        dma((rounds, max(chips - 1, 1), 2)),
        dma((3, wpeers)),
        dma((3, wpeers)),
        dma((rounds, max(chips - 1, 1), wpeers)),
        dma((rounds, max(chips - 1, 1), wpeers)),
        dma((chunks,)),
        dma((chunks,)),
        dma((chunks, peers)),
        dma((chunks, peers)),
        dma((4, rpeers)),
        dma((4, rpeers)),
    ]
    hbm = pl.BlockSpec(memory_space=pl.ANY)
    vmem = pl.BlockSpec(memory_space=pltpu.VMEM)
    layer_shape = jax.ShapeDtypeStruct((samples, d, n), BF16)
    emb_shape = jax.ShapeDtypeStruct((pooled.shape[0], nr, dq), BF16)
    if fused:
        grad_shapes = (jax.ShapeDtypeStruct((pieces, 16, 128), BF16),)
    else:
        grad_shapes = tuple(jax.ShapeDtypeStruct(s, F32) for s in ((jq, n), (kq, n), (kq, d)))
    layer, emb, *grads = pl.pallas_call(
        functools.partial(layer_kernel, cfg),
        out_shape=(layer_shape, emb_shape, *grad_shapes),
        in_specs=[hbm] * 5,
        out_specs=(hbm, hbm) + (vmem,) * len(grad_shapes),
        scratch_shapes=scratch,
        compiler_params=pltpu.CompilerParams(
            collective_id=0, has_side_effects=True, vmem_limit_bytes=VMEM_BYTES
        ),
        name="interaction_layer",
    )(pooled, lc_weight, fm_proj, fm_out.T, cotangent.transpose(0, 2, 1))
    if fused:
        layer, emb, lc_g, proj_g, out_t = pl.pallas_call(
            write_kernel,
            out_shape=(
                layer_shape,
                emb_shape,
                jax.ShapeDtypeStruct((jq, n), F32),
                jax.ShapeDtypeStruct((n, kq), F32),
                jax.ShapeDtypeStruct((d, kq), F32),
            ),
            in_specs=[hbm] * 3,
            out_specs=(hbm,) * 5,
            scratch_shapes=[
                pltpu.VMEM(layer_shape.shape, BF16),
                pltpu.VMEM(emb_shape.shape, BF16),
                pltpu.VMEM(grad_shapes[0].shape, BF16),
                pltpu.VMEM((jq, n), F32),
                pltpu.VMEM((n, kq), F32),
                pltpu.VMEM((d, kq), F32),
                dma((2, 11)),
            ],
            compiler_params=pltpu.CompilerParams(vmem_limit_bytes=VMEM_BYTES),
            name="write_outputs",
        )(layer, emb, *grads)
        out_g = out_t.T
    else:
        lc_g, proj_t, out_g = lax.psum(tuple(grads), ("rep", "table"))
        proj_g = proj_t.T
    return layer.transpose(0, 2, 1), emb, lc_g, proj_g, out_g


def solution(mesh):
    in_specs = (
        P("rep", "table", None),
        P("tensor", None),
        P(None, "tensor"),
        P("tensor", None),
        P(("rep", "table"), None, None),
    )
    out_specs = (
        P(("rep", "table"), None, None),
        P("rep", "table", "tensor"),
        P("tensor", None),
        P(None, "tensor"),
        P("tensor", None),
    )
    return jax.shard_map(
        functools.partial(shards, dict(mesh.shape)),
        mesh=mesh, in_specs=in_specs, out_specs=out_specs, check_vma=False,
    )
```

```python
import functools

import jax
import jax.numpy as jnp
from jax import lax
from jax.experimental import pallas as pl
from jax.experimental.pallas import tpu as pltpu
from jax.sharding import PartitionSpec as P

MESH = pl.DeviceIdType.MESH
BF16 = jnp.bfloat16
F32 = jnp.float32
VMEM_BYTES = 60 * 1024 * 1024


def dot_nn(a, b):
    return jnp.dot(a, b, preferred_element_type=F32)


def layer_kernel(cfg, pooled, lc_w, proj_w, out_w, cot, layer, emb, *rest):
    tables, reps, tensors = cfg["tables"], cfg["reps"], cfg["tensors"]
    samples, nr, n, d = cfg["samples"], cfg["nr"], cfg["n"], cfg["d"]
    kq, jq, dq, cs, pp, fused = cfg["kq"], cfg["jq"], cfg["dq"], cfg["cs"], cfg["pp"], cfg["fused"]
    grads, scratch = (rest[:1], rest[1:]) if fused else (rest[:3], rest[3:])
    (x_ref, gt_ref, g_ref, xt_ref, pw, ww, ow, p_rel, ot_rel, own_ct, own_cgt, own_it, igt, lo, eg, er, xin, xout, acc_l, acc_p, acc_o,
     gb, rb1, sb, rb2, fs, loc, x_send, x_recv, w_send, w_recv, f_send, f_recv, c_send, c_recv, e_out, e_send, e_recv, r_send, r_recv) = scratch
    chunks = samples // cs
    t = lax.axis_index("table")
    r = lax.axis_index("rep")
    x = lax.axis_index("tensor")

    def peer(axis, me, size, j):
        return {axis: lax.rem(me + j, size)}

    barrier = pltpu.get_barrier_semaphore()
    groups = [("table", t, tables), ("tensor", x, tensors)] + ([("rep", r, reps)] if fused else [])
    signals = 0
    for axis, me, size in groups:
        for j in range(1, size):
            pl.semaphore_signal(barrier, inc=1, device_id=peer(axis, me, size, j), device_id_type=MESH)
            signals += 1

    g_load = pltpu.make_async_copy(cot, gt_ref, loc.at[0])

    def x_load(i, to):
        rows = pl.ds(to * samples, samples)
        return pltpu.make_async_copy(pooled.at[rows], xin.at[rows], loc.at[4 + 2 * chunks + i])

    w_pairs = ((proj_w, pw), (out_w, ow), (lc_w, ww))
    w_loads = [
        pltpu.make_async_copy(src, dst.at[x], loc.at[1 + i]) for i, (src, dst) in enumerate(w_pairs)
    ]
    targets = [lax.rem(t + j, tables) for j in range(tables)]
    for i, to in enumerate(targets):
        x_load(i, to).start()
    for load in w_loads:
        load.start()
    g_load.start()
    for i, to in enumerate(targets):
        rows = pl.ds(to * samples, samples)
        x_load(i, to).wait()
        if i == 0:
            x_ref[:, t, :, :d] = xin[rows]
        else:
            xout[rows, :, :d] = xin[rows]
    pl.semaphore_wait(barrier, signals)

    chips, rounds = tables // 2, chunks // tensors
    chip, core = t // 2, lax.rem(t, 2)
    mate = chip * 2 + lax.rem(core + 1, 2)

    def c_copy(c):
        return pltpu.make_async_remote_copy(
            xout.at[pl.ds(mate * samples + c * cs, cs)],
            x_ref.at[pl.ds(c * cs, cs), t],
            c_send.at[c],
            c_recv.at[c],
            device_id={"table": mate},
            device_id_type=MESH,
        )

    def x_copy(g, a, b):
        to = lax.rem(chip + a, chips) * 2 + lax.rem(core + b, 2)
        first_row = (g * tensors + x) * cs
        return pltpu.make_async_remote_copy(
            xout.at[pl.ds(to * samples + first_row, cs)],
            x_ref.at[pl.ds(first_row, cs), t],
            x_send.at[g, a - 1, b],
            x_recv.at[g, a - 1, b],
            device_id={"table": to},
            device_id_type=MESH,
        )

    def f_copy(g, a, j):
        source = lax.rem(chip + chips - a, chips) * 2
        held = x_ref.at[pl.ds((g * tensors + x) * cs, cs), pl.ds(source, 2)]
        return pltpu.make_async_remote_copy(
            held, held, f_send.at[g, a - 1, j - 1], f_recv.at[g, a - 1, j - 1],
            device_id=peer("tensor", x, tensors, j), device_id_type=MESH,
        )

    def pass_on(g):
        for a in range(1, chips):
            for b in range(2):
                x_copy(g, a, b).wait_recv()
            for j in range(1, tensors):
                f_copy(g, a, j).start()

    def w_copy(i, j):
        src, dst = w_pairs[i]
        return pltpu.make_async_remote_copy(
            src, dst.at[x], w_send.at[i, j - 1], w_recv.at[i, j - 1],
            device_id=peer("tensor", x, tensors, j), device_id_type=MESH,
        )

    for g in range(rounds):
        for a in range(1, chips):
            for b in range(2):
                x_copy(g, a, b).start()
    for c in range(chunks):
        c_copy(c).start()
    for j in range(1, tensors):
        for i in range(3):
            w_copy(i, j).start()

    for load in w_loads:
        load.wait()
    own_pt, own_o = pw[x].T, ow[x].T
    acc_l[...] = jnp.zeros_like(acc_l)
    acc_p[...] = jnp.zeros_like(acc_p)
    acc_o[...] = jnp.zeros_like(acc_o)
    g_load.wait()

    def before(c, carry):
        at = [c * cs + i for i in range(cs)]
        for s in at:
            gt = gt_ref[s]
            g_ref[s] = gt.T
            igt[s] = dot_nn(own_o, gt).astype(BF16)
        return carry

    lax.fori_loop(0, chunks, before, 0)

    def first(c):
        at = [c * cs + i for i in range(cs)]
        own_rows = [x_ref[s, pl.ds(x * (jq // nr), jq // nr), :, :d].reshape(jq, d) for s in at]
        xs = [x_ref[s, :, :, :d].reshape(n, d) for s in at]
        xt = [v.T for v in xs]
        comp = [dot_nn(own_pt, v).astype(BF16) for v in xs]
        cgrad = [dot_nn(igt[s], v).astype(BF16) for s, v in zip(at, xs)]
        sum_l = acc_l[...]
        for s, v in zip(at, own_rows):
            sum_l = sum_l + dot_nn(v, gt_ref[s])
        inter = [dot_nn(v, w).astype(BF16) for v, w in zip(comp, xt)]
        sum_p = acc_p[...]
        for v, w in zip(cgrad, xt):
            sum_p = sum_p + dot_nn(v, w)
        sum_o = acc_o[:, :d]
        for s, v in zip(at, inter):
            sum_o = sum_o + dot_nn(v, g_ref[s])
        acc_l[...] = sum_l
        acc_p[...] = sum_p
        acc_o[:, :d] = sum_o
        for i, s in enumerate(at):
            xt_ref[s] = xt[i]
            own_ct[s] = comp[i]
            own_cgt[s] = cgrad[i]
            own_it[s] = inter[i]

    for c in range(chunks):
        c_copy(c).wait_recv()
    pass_on(0)
    for g in range(rounds):
        first(g * tensors + x)
        if g + 1 < rounds:
            pass_on(g + 1)
        for j in range(1, tensors):
            for a in range(1, chips):
                f_copy(g, a, j).wait_recv()
            first(g * tensors + lax.rem(x + tensors - j, tensors))

    part = reps * pp

    def rs_table(j):
        to = lax.rem(t + j, tables)
        return pltpu.make_async_remote_copy(
            gb.at[pl.ds(to * part, part)], rb1.at[j - 1], r_send.at[0, j - 1], r_recv.at[0, j - 1],
            device_id=peer("table", t, tables, j), device_id_type=MESH,
        )

    def rs_rep(j):
        to = lax.rem(r + j, reps)
        return pltpu.make_async_remote_copy(
            sb.at[pl.ds(to * pp, pp)], rb2.at[j - 1], r_send.at[1, j - 1], r_recv.at[1, j - 1],
            device_id=peer("rep", r, reps, j), device_id_type=MESH,
        )

    def ag_rep(j):
        mine = fs.at[pl.ds(t * part + r * pp, pp)]
        return pltpu.make_async_remote_copy(
            mine, mine, r_send.at[2, j - 1], r_recv.at[2, j - 1],
            device_id=peer("rep", r, reps, j), device_id_type=MESH,
        )

    def ag_table(j):
        mine = fs.at[pl.ds(t * part, part)]
        return pltpu.make_async_remote_copy(
            mine, mine, r_send.at[3, j - 1], r_recv.at[3, j - 1],
            device_id=peer("table", t, tables, j), device_id_type=MESH,
        )

    layout = ((acc_l, jq, cfg["wide_scale"]), (acc_p, kq, cfg["wide_scale"]), (acc_o, kq, cfg["out_scale"]))
    if fused:
        at = 0
        for ref, rows, scale in layout:
            for h in range(n // 128):
                value = (ref[:, h * 128:(h + 1) * 128] * scale).astype(BF16)
                gb[at:at + rows // 16] = value.reshape(rows // 16, 16, 128)
                at += rows // 16
        for j in range(1, tables):
            rs_table(j).start()

    def reduce_step(c):
        if not fused:
            return

        @pl.when(c == 0)
        def _():
            total = gb[pl.ds(t * part, part)].astype(F32)
            for j in range(1, tables):
                rs_table(j).wait_recv()
                total = total + rb1[j - 1].astype(F32)
            sb[...] = total.astype(BF16)
            for j in range(1, reps):
                rs_rep(j).start()

        @pl.when(c == 1)
        def _():
            total = sb[pl.ds(r * pp, pp)].astype(F32)
            for j in range(1, reps):
                rs_rep(j).wait_recv()
                total = total + rb2[j - 1].astype(F32)
            fs[pl.ds(t * part + r * pp, pp)] = total.astype(BF16)
            for j in range(1, reps):
                ag_rep(j).start()

        @pl.when(c == 2)
        def _():
            for j in range(1, reps):
                ag_rep(j).wait_recv()
            for j in range(1, tables):
                ag_table(j).start()

    for j in range(1, tensors):
        for i in range(3):
            w_copy(i, j).wait_recv()
    order = [x] + [lax.rem(x + j, tensors) for j in range(1, tensors)]
    p_rel[...] = jnp.concatenate([pw[q] for q in order], axis=1)
    ot_rel[...] = jnp.concatenate([ow[q] for q in order], axis=1)
    other_pt = [pw[q].T for q in order[1:]]
    other_o = [ow[q].T for q in order[1:]]

    def lo_store(c):
        rows = pl.ds(c * cs, cs)
        return pltpu.make_async_copy(lo.at[rows], layer.at[rows], loc.at[4 + c])

    def e_store(c):
        return pltpu.make_async_copy(
            eg.at[pl.ds(c * cs, cs), t], emb.at[pl.ds(t * samples + c * cs, cs)], loc.at[4 + chunks + c]
        )

    def e_copy(c, j):
        to = lax.rem(t + j, tables)
        return pltpu.make_async_remote_copy(
            eg.at[pl.ds(c * cs, cs), to],
            er.at[pl.ds(t * samples + c * cs, cs)],
            e_send.at[c, j - 1],
            e_recv.at[c, j - 1],
            device_id=peer("table", t, tables, j),
            device_id_type=MESH,
        )

    def second(c, carry):
        at = [c * cs + i for i in range(cs)]
        xs = [x_ref[s, :, :, :d].reshape(n, d) for s in at]
        w_all = ww[...].reshape(n, n)
        igrad_t = [[dot_nn(v, gt_ref[s]).astype(BF16) for v in other_o] for s in at]
        comp = [[dot_nn(v, w).astype(BF16) for v in other_pt] for w in xs]
        igrad = [dot_nn(g_ref[s], ot_rel[...]).astype(BF16) for s in at]
        cgrad = [[dot_nn(v, w).astype(BF16) for v in vs] for vs, w in zip(igrad_t, xs)]
        inter = [[dot_nn(v, xt_ref[s]).astype(BF16) for v in vs] for vs, s in zip(comp, at)]
        for i, s in enumerate(at):
            gs = g_ref[s]
            left = jnp.concatenate([igrad[i], p_rel[...], w_all], axis=1)
            right = jnp.concatenate([own_ct[s], *comp[i], own_cgt[s], *cgrad[i], gs], axis=0)
            grad = dot_nn(left, right) + gs.astype(F32)
            own = grad[:, :dq]
            for q in range(1, tensors):
                own = jnp.where(x == q, grad[:, q * dq:(q + 1) * dq], own)
            eg[s, :, :, :dq] = own.reshape(tables, nr, dq).astype(BF16)
        for j in range(1, tables):
            e_copy(c, j).start()
        e_store(c).start()
        for i, s in enumerate(at):
            xt = xt_ref[s]
            left = jnp.concatenate([ot_rel[...], xt], axis=1)
            right = jnp.concatenate([own_it[s], *inter[i], w_all], axis=0)
            lo[s] = (dot_nn(left, right) + xt.astype(F32)).astype(BF16)
        lo_store(c).start()
        reduce_step(c)
        return carry

    lax.fori_loop(0, chunks, second, 0)

    def er_store(c, j):
        rows = pl.ds(lax.rem(t + tables - j, tables) * samples + c * cs, cs)
        return pltpu.make_async_copy(er.at[rows], emb.at[rows], e_out.at[c, j - 1])

    for c in range(chunks):
        for j in range(1, tables):
            e_copy(c, j).wait_recv()
            er_store(c, j).start()

    if fused:
        for j in range(1, tables):
            ag_table(j).wait_recv()
        grads[0][...] = fs[...]
    else:
        for ref, (acc, rows, scale) in zip(grads, layout):
            ref[...] = acc[:, :ref.shape[1]] * scale

    for c in range(chunks):
        lo_store(c).wait()
        e_store(c).wait()
        for j in range(1, tables):
            er_store(c, j).wait()
    for c in range(chunks):
        c_copy(c).wait_send()
        for j in range(1, tables):
            e_copy(c, j).wait_send()
    for g in range(rounds):
        for a in range(1, chips):
            for b in range(2):
                x_copy(g, a, b).wait_send()
            for j in range(1, tensors):
                f_copy(g, a, j).wait_send()
    for j in range(1, tensors):
        for i in range(3):
            w_copy(i, j).wait_send()
    if fused:
        for j in range(1, tables):
            rs_table(j).wait_send()
            ag_table(j).wait_send()
        for j in range(1, reps):
            rs_rep(j).wait_send()
            ag_rep(j).wait_send()


def write_kernel(layer, emb, pieces, layer_out, emb_out, lc_g, proj_g, out_g,
                 held_l, held_e, narrow_e, held_g, lc_v, proj_v, out_v, sems):
    g_load = pltpu.make_async_copy(pieces, held_g, sems.at[0, 8])
    g_load.start()
    loads, stores = [], []
    dq = emb_out.shape[2]
    for src, held, ready, dst in ((emb, held_e, narrow_e, emb_out), (layer, held_l, held_l, layer_out)):
        parts = 4 if src.shape[0] % 4 == 0 else 1
        size = src.shape[0] // parts
        for p in range(parts):
            rows = pl.ds(p * size, size)
            at = len(loads)
            loads.append(pltpu.make_async_copy(src.at[rows], held.at[rows], sems.at[0, at]))
            stores.append((rows, ready is held, pltpu.make_async_copy(ready.at[rows], dst.at[rows], sems.at[1, at])))
    for load in loads:
        load.start()
    g_load.wait()
    at = 0
    wide = []
    for rows in (lc_g.shape[0], proj_g.shape[1], out_g.shape[1]):
        halves = []
        for _ in range(lc_g.shape[1] // 128):
            halves.append(held_g[at:at + rows // 16].reshape(rows, 128).astype(F32))
            at += rows // 16
        wide.append(halves)
    lc_v[...] = jnp.concatenate(wide[0], axis=1)
    proj_v[...] = jnp.concatenate([half.T for half in wide[1]], axis=0)
    out_v[...] = jnp.concatenate([half.T for half in wide[2]], axis=0)[:out_g.shape[0]]
    grads = [
        pltpu.make_async_copy(held, dst, sems.at[1, 8 + i])
        for i, (held, dst) in enumerate(((lc_v, lc_g), (proj_v, proj_g), (out_v, out_g)))
    ]
    for store in grads:
        store.start()
    for load, (rows, whole, store) in zip(loads, stores):
        load.wait()
        if not whole:
            narrow_e[rows] = held_e[rows, :, :dq]
        store.start()
    for store in grads + [store for _, _, store in stores]:
        store.wait()


def shards(sizes, pooled, lc_weight, fm_proj, fm_out, cotangent):
    tables, reps, tensors = sizes["table"], sizes["rep"], sizes["tensor"]
    samples, n, d = cotangent.shape
    nr = pooled.shape[1]
    jq, kq, dq = lc_weight.shape[0], fm_out.shape[0], d // tensors
    total = samples * reps * tables
    cs = 2 if samples % (2 * tensors) == 0 else 1
    chunks = samples // cs
    rounds, chips = chunks // tensors, tables // 2
    wide, dq_wide = -(-d // 128) * 128, -(-dq // 128) * 128
    pieces = (n // 128) * (jq // 16 + kq // 16) + (wide // 128) * (kq // 16)
    group = tables * reps
    fused = pieces % group == 0 and wide == n and jq % 16 == 0 and kq % 16 == 0
    pp = pieces // group if fused else 1
    cfg = dict(
        tables=tables, reps=reps, tensors=tensors, samples=samples, nr=nr, n=n, d=d, kq=kq, jq=jq, dq=dq,
        cs=cs, pp=pp, fused=fused,
        wide_scale=float(total * d) ** (-0.5), out_scale=float(total * n * d) ** (-0.5),
    )
    part = reps * pp if fused else 1
    held = pieces if fused else 1
    dma = pltpu.SemaphoreType.DMA
    peers = max(tables - 1, 1)
    wpeers = max(tensors - 1, 1)
    rpeers = max(tables - 1, reps - 1, 1)
    k = kq * tensors
    scratch = [
        pltpu.VMEM((samples, tables, nr, wide), BF16),
        pltpu.VMEM((samples, d, n), BF16),
        pltpu.VMEM((samples, n, d), BF16),
        pltpu.VMEM((samples, d, n), BF16),
        pltpu.VMEM((tensors, n, kq), BF16),
        pltpu.VMEM((tensors, jq, n), BF16),
        pltpu.VMEM((tensors, d, kq), BF16),
        pltpu.VMEM((n, k), BF16),
        pltpu.VMEM((d, k), BF16),
        pltpu.VMEM((samples, kq, d), BF16),
        pltpu.VMEM((samples, kq, d), BF16),
        pltpu.VMEM((samples, kq, n), BF16),
        pltpu.VMEM((samples, kq, n), BF16),
        pltpu.VMEM((samples, d, n), BF16),
        pltpu.VMEM((samples, tables, nr, dq_wide), BF16),
        pltpu.VMEM((tables * samples, nr, dq_wide), BF16),
        pltpu.VMEM((tables * samples, nr, d), BF16),
        pltpu.VMEM((tables * samples, nr, wide), BF16),
        pltpu.VMEM((jq, n), F32),
        pltpu.VMEM((kq, n), F32),
        pltpu.VMEM((kq, wide), F32),
        pltpu.VMEM((held, 16, 128), BF16),
        pltpu.VMEM((peers, part, 16, 128), BF16),
        pltpu.VMEM((part, 16, 128), BF16),
        pltpu.VMEM((max(reps - 1, 1), pp, 16, 128), BF16),
        pltpu.VMEM((held, 16, 128), BF16),
        dma((2 * chunks + 4 + tables,)),
        dma((rounds, max(chips - 1, 1), 2)),
        dma((rounds, max(chips - 1, 1), 2)),
        dma((3, wpeers)),
        dma((3, wpeers)),
        dma((rounds, max(chips - 1, 1), wpeers)),
        dma((rounds, max(chips - 1, 1), wpeers)),
        dma((chunks,)),
        dma((chunks,)),
        dma((chunks, peers)),
        dma((chunks, peers)),
        dma((chunks, peers)),
        dma((4, rpeers)),
        dma((4, rpeers)),
    ]
    hbm = pl.BlockSpec(memory_space=pl.ANY)
    vmem = pl.BlockSpec(memory_space=pltpu.VMEM)
    layer_shape = jax.ShapeDtypeStruct((samples, d, n), BF16)
    emb_shape = jax.ShapeDtypeStruct((pooled.shape[0], nr, dq), BF16)
    emb_wide = jax.ShapeDtypeStruct((pooled.shape[0], nr, dq_wide), BF16)
    if fused:
        grad_shapes = (jax.ShapeDtypeStruct((pieces, 16, 128), BF16),)
    else:
        grad_shapes = tuple(jax.ShapeDtypeStruct(s, F32) for s in ((jq, n), (kq, n), (kq, d)))
    layer, emb, *grads = pl.pallas_call(
        functools.partial(layer_kernel, cfg),
        out_shape=(layer_shape, emb_wide, *grad_shapes),
        in_specs=[hbm] * 5,
        out_specs=(hbm, hbm) + (vmem,) * len(grad_shapes),
        scratch_shapes=scratch,
        compiler_params=pltpu.CompilerParams(
            collective_id=0, has_side_effects=True, vmem_limit_bytes=VMEM_BYTES
        ),
        name="interaction_layer",
    )(pooled, lc_weight, fm_proj, fm_out.T, cotangent.transpose(0, 2, 1))
    if fused:
        layer, emb, lc_g, proj_g, out_t = pl.pallas_call(
            write_kernel,
            out_shape=(
                layer_shape,
                emb_shape,
                jax.ShapeDtypeStruct((jq, n), F32),
                jax.ShapeDtypeStruct((n, kq), F32),
                jax.ShapeDtypeStruct((d, kq), F32),
            ),
            in_specs=[hbm] * 3,
            out_specs=(hbm,) * 5,
            scratch_shapes=[
                pltpu.VMEM(layer_shape.shape, BF16),
                pltpu.VMEM(emb_wide.shape, BF16),
                pltpu.VMEM(emb_shape.shape, BF16),
                pltpu.VMEM(grad_shapes[0].shape, BF16),
                pltpu.VMEM((jq, n), F32),
                pltpu.VMEM((n, kq), F32),
                pltpu.VMEM((d, kq), F32),
                dma((2, 11)),
            ],
            compiler_params=pltpu.CompilerParams(vmem_limit_bytes=VMEM_BYTES),
            name="write_outputs",
        )(layer, emb, *grads)
        out_g = out_t.T
    else:
        lc_g, proj_t, out_g = lax.psum(tuple(grads), ("rep", "table"))
        proj_g = proj_t.T
        emb = emb[:, :, :dq]
    return layer.transpose(0, 2, 1), emb, lc_g, proj_g, out_g


def solution(mesh):
    in_specs = (
        P("rep", "table", None),
        P("tensor", None),
        P(None, "tensor"),
        P("tensor", None),
        P(("rep", "table"), None, None),
    )
    out_specs = (
        P(("rep", "table"), None, None),
        P("rep", "table", "tensor"),
        P("tensor", None),
        P(None, "tensor"),
        P("tensor", None),
    )
    return jax.shard_map(
        functools.partial(shards, dict(mesh.shape)),
        mesh=mesh, in_specs=in_specs, out_specs=out_specs, check_vma=False,
    )
```

```python
import functools

import jax
import jax.numpy as jnp
from jax import lax
from jax.experimental import pallas as pl
from jax.experimental.pallas import tpu as pltpu
from jax.sharding import PartitionSpec as P

MESH = pl.DeviceIdType.MESH
BF16 = jnp.bfloat16
F32 = jnp.float32
VMEM_BYTES = 60 * 1024 * 1024


def dot_nn(a, b):
    return jnp.dot(a, b, preferred_element_type=F32)


def dot_nt(a, b):
    return lax.dot_general(a, b, (((1,), (1,)), ((), ())), preferred_element_type=F32)


def layer_kernel(cfg, pooled, lc_w, proj_w, out_w, cot, layer, emb, *rest):
    tables, reps, tensors = cfg["tables"], cfg["reps"], cfg["tensors"]
    samples, nr, n, d = cfg["samples"], cfg["nr"], cfg["n"], cfg["d"]
    kq, jq, dq, cs, pp, fused = cfg["kq"], cfg["jq"], cfg["dq"], cfg["cs"], cfg["pp"], cfg["fused"]
    grads, scratch = (rest[:1], rest[1:]) if fused else (rest[:3], rest[3:])
    (x_ref, gt_ref, g_ref, pw, ww, ow, p_rel, ot_rel, o_rel, w_t, back, c_ref, cg_ref, i_ref, ig_ref, lo, eg, acc_l, acc_p, acc_o,
     gb, rb1, sb, rb2, fs, loc, x_send, x_recv, w_send, w_recv, f_send, f_recv, c_send, c_recv, e_send, e_recv, r_send, r_recv) = scratch
    chunks, k = samples // cs, tensors * kq
    t = lax.axis_index("table")
    r = lax.axis_index("rep")
    x = lax.axis_index("tensor")

    def peer(axis, me, size, j):
        return {axis: lax.rem(me + j, size)}

    barrier = pltpu.get_barrier_semaphore()
    groups = [("table", t, tables), ("tensor", x, tensors)] + ([("rep", r, reps)] if fused else [])
    signals = 0
    for axis, me, size in groups:
        for j in range(1, size):
            pl.semaphore_signal(barrier, inc=1, device_id=peer(axis, me, size, j), device_id_type=MESH)
            signals += 1

    g_load = pltpu.make_async_copy(cot, gt_ref, loc.at[chunks])

    def x_load(c):
        return pltpu.make_async_copy(
            pooled.at[pl.ds(t * samples + c * cs, cs)], x_ref.at[pl.ds(c * cs, cs), t], loc.at[c]
        )

    w_pairs = ((proj_w, pw), (out_w, ow), (lc_w, ww))
    w_loads = [
        pltpu.make_async_copy(src, dst.at[x], loc.at[chunks + 1 + i]) for i, (src, dst) in enumerate(w_pairs)
    ]
    for load in w_loads:
        load.start()
    g_load.start()
    for c in range(chunks):
        x_load(c).start()
    pl.semaphore_wait(barrier, signals)

    chips, rounds = tables // 2, chunks // tensors
    chip, core = t // 2, lax.rem(t, 2)
    mate = chip * 2 + lax.rem(core + 1, 2)

    def c_copy(c):
        return pltpu.make_async_remote_copy(
            pooled.at[pl.ds(mate * samples + c * cs, cs)],
            x_ref.at[pl.ds(c * cs, cs), t],
            c_send.at[c],
            c_recv.at[c],
            device_id={"table": mate},
            device_id_type=MESH,
        )

    def x_copy(g, a, b):
        to = lax.rem(chip + a, chips) * 2 + lax.rem(core + b, 2)
        first_row = (g * tensors + x) * cs
        return pltpu.make_async_remote_copy(
            pooled.at[pl.ds(to * samples + first_row, cs)],
            x_ref.at[pl.ds(first_row, cs), t],
            x_send.at[g, a - 1, b],
            x_recv.at[g, a - 1, b],
            device_id={"table": to},
            device_id_type=MESH,
        )

    def f_copy(g, a, j):
        source = lax.rem(chip + chips - a, chips) * 2
        held = x_ref.at[pl.ds((g * tensors + x) * cs, cs), pl.ds(source, 2)]
        return pltpu.make_async_remote_copy(
            held, held, f_send.at[g, a - 1, j - 1], f_recv.at[g, a - 1, j - 1],
            device_id=peer("tensor", x, tensors, j), device_id_type=MESH,
        )

    def pass_on(g):
        for a in range(1, chips):
            for b in range(2):
                x_copy(g, a, b).wait_recv()
            for j in range(1, tensors):
                f_copy(g, a, j).start()

    def w_copy(i, j):
        src, dst = w_pairs[i]
        return pltpu.make_async_remote_copy(
            src, dst.at[x], w_send.at[i, j - 1], w_recv.at[i, j - 1],
            device_id=peer("tensor", x, tensors, j), device_id_type=MESH,
        )

    for j in range(1, tensors):
        for i in range(3):
            w_copy(i, j).start()
    for g in range(rounds):
        for a in range(1, chips):
            for b in range(2):
                x_copy(g, a, b).start()
    for c in range(chunks):
        c_copy(c).start()

    acc_l[...] = jnp.zeros_like(acc_l)
    acc_p[...] = jnp.zeros_like(acc_p)
    acc_o[...] = jnp.zeros_like(acc_o)
    g_load.wait()
    for s in range(samples):
        g_ref[s] = gt_ref[s].T
    for load in w_loads:
        load.wait()
    for j in range(1, tensors):
        for i in range(2):
            w_copy(i, j).wait_recv()
    order = [x] + [lax.rem(x + j, tensors) for j in range(1, tensors)]
    p_rel[...] = jnp.concatenate([pw[q] for q in order], axis=1)
    ot_rel[...] = jnp.concatenate([ow[q] for q in order], axis=1)
    o_rel[...] = ot_rel[...].T
    back[:k] = p_rel[...].T

    def before(c, carry):
        rows = pl.ds(c * cs, cs)
        igrad = dot_nn(g_ref[rows].reshape(cs * n, d), ot_rel[...])
        ig_ref[rows] = igrad.astype(BF16).reshape(cs, n, k)
        return carry

    lax.fori_loop(0, chunks, before, 0)

    def first(c):
        at = [c * cs + i for i in range(cs)]
        own_rows = [x_ref[s, pl.ds(x * (jq // nr), jq // nr)].reshape(jq, d) for s in at]
        xs = [x_ref[s].reshape(n, d) for s in at]
        xt = [v.T for v in xs]
        comp = dot_nn(jnp.concatenate(xt, axis=0), p_rel[...]).astype(BF16)
        comp = [comp[i * d:(i + 1) * d] for i in range(cs)]
        cgrad = [dot_nn(v, ig_ref[s]).astype(BF16) for s, v in zip(at, xt)]
        sum_l = acc_l[...]
        for s, v in zip(at, own_rows):
            sum_l = sum_l + dot_nn(v, gt_ref[s])
        inter = [dot_nn(v, w).astype(BF16) for v, w in zip(xs, comp)]
        sum_p = acc_p[...]
        for v, w in zip(xs, cgrad):
            sum_p = sum_p + dot_nn(v, w[:, :kq])
        sum_o = acc_o[:d]
        for s, v in zip(at, inter):
            sum_o = sum_o + dot_nn(gt_ref[s], v[:, :kq])
        acc_l[...] = sum_l
        acc_p[...] = sum_p
        acc_o[:d] = sum_o
        for i, s in enumerate(at):
            c_ref[s] = comp[i]
            cg_ref[s] = cgrad[i]
            i_ref[s] = inter[i]

    for c in range(chunks):
        x_load(c).wait()
        c_copy(c).wait_recv()
    pass_on(0)
    for g in range(rounds):
        first(g * tensors + x)
        if g + 1 < rounds:
            pass_on(g + 1)
        for j in range(1, tensors):
            for a in range(1, chips):
                f_copy(g, a, j).wait_recv()
            first(g * tensors + lax.rem(x + tensors - j, tensors))

    part = reps * pp

    def rs_table(j):
        to = lax.rem(t + j, tables)
        return pltpu.make_async_remote_copy(
            gb.at[pl.ds(to * part, part)], rb1.at[j - 1], r_send.at[0, j - 1], r_recv.at[0, j - 1],
            device_id=peer("table", t, tables, j), device_id_type=MESH,
        )

    def rs_rep(j):
        to = lax.rem(r + j, reps)
        return pltpu.make_async_remote_copy(
            sb.at[pl.ds(to * pp, pp)], rb2.at[j - 1], r_send.at[1, j - 1], r_recv.at[1, j - 1],
            device_id=peer("rep", r, reps, j), device_id_type=MESH,
        )

    def ag_rep(j):
        mine = fs.at[pl.ds(t * part + r * pp, pp)]
        return pltpu.make_async_remote_copy(
            mine, mine, r_send.at[2, j - 1], r_recv.at[2, j - 1],
            device_id=peer("rep", r, reps, j), device_id_type=MESH,
        )

    def ag_table(j):
        mine = fs.at[pl.ds(t * part, part)]
        return pltpu.make_async_remote_copy(
            mine, mine, r_send.at[3, j - 1], r_recv.at[3, j - 1],
            device_id=peer("table", t, tables, j), device_id_type=MESH,
        )

    layout = ((acc_l, cfg["wide_scale"]), (acc_p, cfg["wide_scale"]), (acc_o, cfg["out_scale"]))
    if fused:
        at = 0
        for ref, scale in layout:
            rows = ref.shape[0]
            for h in range(ref.shape[1] // 128):
                value = (ref[:, h * 128:(h + 1) * 128] * scale).astype(BF16)
                gb[at:at + rows // 16] = value.reshape(rows // 16, 16, 128)
                at += rows // 16
        for j in range(1, tables):
            rs_table(j).start()

    def reduce_step(c):
        if not fused:
            return

        @pl.when(c == 0)
        def _():
            total = gb[pl.ds(t * part, part)].astype(F32)
            for j in range(1, tables):
                rs_table(j).wait_recv()
                total = total + rb1[j - 1].astype(F32)
            sb[...] = total.astype(BF16)
            for j in range(1, reps):
                rs_rep(j).start()

        @pl.when(c == 1)
        def _():
            total = sb[pl.ds(r * pp, pp)].astype(F32)
            for j in range(1, reps):
                rs_rep(j).wait_recv()
                total = total + rb2[j - 1].astype(F32)
            fs[pl.ds(t * part + r * pp, pp)] = total.astype(BF16)
            for j in range(1, reps):
                ag_rep(j).start()

        @pl.when(c == 2)
        def _():
            for j in range(1, reps):
                ag_rep(j).wait_recv()
            for j in range(1, tables):
                ag_table(j).start()

    for j in range(1, tensors):
        w_copy(2, j).wait_recv()
    w_t[...] = ww[...].reshape(n, n).T
    back[k:] = w_t[...]
    own_d = pl.ds(pl.multiple_of(x * dq, dq), dq)

    def lo_store(c):
        rows = pl.ds(c * cs, cs)
        return pltpu.make_async_copy(lo.at[rows], layer.at[rows], loc.at[chunks + 4 + c])

    def e_store(c):
        return pltpu.make_async_copy(
            eg.at[pl.ds(c * cs, cs), t], emb.at[pl.ds(t * samples + c * cs, cs)], loc.at[2 * chunks + 4 + c]
        )

    def e_copy(c, j):
        to = lax.rem(t + j, tables)
        return pltpu.make_async_remote_copy(
            eg.at[pl.ds(c * cs, cs), to],
            emb.at[pl.ds(t * samples + c * cs, cs)],
            e_send.at[c, j - 1],
            e_recv.at[c, j - 1],
            device_id=peer("table", t, tables, j),
            device_id_type=MESH,
        )

    def second(c, carry):
        at = [c * cs + i for i in range(cs)]
        rows = pl.ds(c * cs, cs)
        gt = gt_ref[rows, own_d]
        left = jnp.concatenate([cg_ref[rows, own_d].reshape(cs * dq, k), gt.reshape(cs * dq, n)], axis=1)
        shared = dot_nn(left, back[...]) + gt.astype(F32).reshape(cs * dq, n)
        terms = [dot_nt(c_ref[s, own_d], ig_ref[s]) for s in at]
        for i, s in enumerate(at):
            grad = shared[i * dq:(i + 1) * dq] + terms[i]
            eg[s] = grad.T.reshape(tables, nr, dq).astype(BF16)
        for j in range(1, tables):
            e_copy(c, j).start()
        e_store(c).start()
        mixture = dot_nn(i_ref[rows].reshape(cs * n, k), o_rel[...])
        xs = [x_ref[s].reshape(n, d) for s in at]
        mixed = [dot_nn(w_t[...], v) for v in xs]
        for i, s in enumerate(at):
            out = xs[i].astype(F32) + (mixture[i * n:(i + 1) * n] + mixed[i])
            lo[s] = out.astype(BF16).T
        lo_store(c).start()
        reduce_step(c)
        return carry

    lax.fori_loop(0, chunks, second, 0)

    if fused:
        for j in range(1, tables):
            ag_table(j).wait_recv()
        grads[0][...] = fs[...]
    else:
        for ref, (acc, scale) in zip(grads, layout):
            ref[...] = acc[:ref.shape[0]] * scale

    for c in range(chunks):
        lo_store(c).wait()
        e_store(c).wait()
        for j in range(1, tables):
            e_copy(c, j).wait_recv()
    for c in range(chunks):
        c_copy(c).wait_send()
        for j in range(1, tables):
            e_copy(c, j).wait_send()
    for g in range(rounds):
        for a in range(1, chips):
            for b in range(2):
                x_copy(g, a, b).wait_send()
            for j in range(1, tensors):
                f_copy(g, a, j).wait_send()
    for j in range(1, tensors):
        for i in range(3):
            w_copy(i, j).wait_send()
    if fused:
        for j in range(1, tables):
            rs_table(j).wait_send()
            ag_table(j).wait_send()
        for j in range(1, reps):
            rs_rep(j).wait_send()
            ag_rep(j).wait_send()


def write_kernel(layer, emb, pieces, layer_out, emb_out, lc_g, proj_g, out_g,
                 held_l, held_e, held_g, lc_v, proj_v, out_v, sems):
    g_load = pltpu.make_async_copy(pieces, held_g, sems.at[0, 8])
    g_load.start()
    loads, stores = [], []
    for src, held, dst in ((layer, held_l, layer_out), (emb, held_e, emb_out)):
        parts = 4 if src.shape[0] % 4 == 0 else 1
        size = src.shape[0] // parts
        for p in range(parts):
            rows = pl.ds(p * size, size)
            at = len(loads)
            loads.append(pltpu.make_async_copy(src.at[rows], held.at[rows], sems.at[0, at]))
            stores.append(pltpu.make_async_copy(held.at[rows], dst.at[rows], sems.at[1, at]))
    for load in loads:
        load.start()
    g_load.wait()
    at = 0
    for ref, rows in ((lc_v, lc_v.shape[0]), (proj_v, proj_v.shape[0]), (out_v, out_v.shape[0])):
        padded = -(-rows // 128) * 128
        for h in range(ref.shape[1] // 128):
            ref[:, h * 128:(h + 1) * 128] = held_g[at:at + rows // 16].reshape(rows, 128).astype(F32)
            at += padded // 16
    for i, (held, dst) in enumerate(((lc_v, lc_g), (proj_v, proj_g), (out_v, out_g))):
        stores.append(pltpu.make_async_copy(held, dst, sems.at[1, 8 + i]))
        stores[-1].start()
    for load, store in zip(loads, stores):
        load.wait()
        store.start()
    for store in stores:
        store.wait()


def shards(sizes, pooled, lc_weight, fm_proj, fm_out, cotangent):
    tables, reps, tensors = sizes["table"], sizes["rep"], sizes["tensor"]
    samples, n, d = cotangent.shape
    nr = pooled.shape[1]
    jq, kq, dq = lc_weight.shape[0], fm_out.shape[0], d // tensors
    total = samples * reps * tables
    cs = 2 if samples % (2 * tensors) == 0 else 1
    chunks = samples // cs
    rounds, chips = chunks // tensors, tables // 2
    wide = -(-d // 128) * 128
    pieces = (n // 128) * (jq // 16) + (kq // 128) * (n // 16 + wide // 16)
    group = tables * reps
    fused = pieces % group == 0 and n % 128 == 0 and jq % 128 == 0 and kq % 128 == 0
    pp = pieces // group if fused else 1
    cfg = dict(
        tables=tables, reps=reps, tensors=tensors, samples=samples, nr=nr, n=n, d=d, kq=kq, jq=jq, dq=dq,
        cs=cs, pp=pp, fused=fused,
        wide_scale=float(total * d) ** (-0.5), out_scale=float(total * n * d) ** (-0.5),
    )
    part = reps * pp if fused else 1
    held = pieces if fused else 1
    dma = pltpu.SemaphoreType.DMA
    peers = max(tables - 1, 1)
    wpeers = max(tensors - 1, 1)
    rpeers = max(tables - 1, reps - 1, 1)
    k = kq * tensors
    scratch = [
        pltpu.VMEM((samples, tables, nr, d), BF16),
        pltpu.VMEM((samples, d, n), BF16),
        pltpu.VMEM((samples, n, d), BF16),
        pltpu.VMEM((tensors, n, kq), BF16),
        pltpu.VMEM((tensors, jq, n), BF16),
        pltpu.VMEM((tensors, d, kq), BF16),
        pltpu.VMEM((n, k), BF16),
        pltpu.VMEM((d, k), BF16),
        pltpu.VMEM((k, d), BF16),
        pltpu.VMEM((n, n), BF16),
        pltpu.VMEM((k + n, n), BF16),
        pltpu.VMEM((samples, d, k), BF16),
        pltpu.VMEM((samples, d, k), BF16),
        pltpu.VMEM((samples, n, k), BF16),
        pltpu.VMEM((samples, n, k), BF16),
        pltpu.VMEM((samples, d, n), BF16),
        pltpu.VMEM((samples, tables, nr, dq), BF16),
        pltpu.VMEM((jq, n), F32),
        pltpu.VMEM((n, kq), F32),
        pltpu.VMEM((wide, kq), F32),
        pltpu.VMEM((held, 16, 128), BF16),
        pltpu.VMEM((peers, part, 16, 128), BF16),
        pltpu.VMEM((part, 16, 128), BF16),
        pltpu.VMEM((max(reps - 1, 1), pp, 16, 128), BF16),
        pltpu.VMEM((held, 16, 128), BF16),
        dma((3 * chunks + 4,)),
        dma((rounds, max(chips - 1, 1), 2)),
        dma((rounds, max(chips - 1, 1), 2)),
        dma((3, wpeers)),
        dma((3, wpeers)),
        dma((rounds, max(chips - 1, 1), wpeers)),
        dma((rounds, max(chips - 1, 1), wpeers)),
        dma((chunks,)),
        dma((chunks,)),
        dma((chunks, peers)),
        dma((chunks, peers)),
        dma((4, rpeers)),
        dma((4, rpeers)),
    ]
    hbm = pl.BlockSpec(memory_space=pl.ANY)
    vmem = pl.BlockSpec(memory_space=pltpu.VMEM)
    layer_shape = jax.ShapeDtypeStruct((samples, d, n), BF16)
    emb_shape = jax.ShapeDtypeStruct((pooled.shape[0], nr, dq), BF16)
    if fused:
        grad_shapes = (jax.ShapeDtypeStruct((pieces, 16, 128), BF16),)
    else:
        grad_shapes = tuple(jax.ShapeDtypeStruct(s, F32) for s in ((jq, n), (n, kq), (d, kq)))
    layer, emb, *grads = pl.pallas_call(
        functools.partial(layer_kernel, cfg),
        out_shape=(layer_shape, emb_shape, *grad_shapes),
        in_specs=[hbm] * 5,
        out_specs=(hbm, hbm) + (vmem,) * len(grad_shapes),
        scratch_shapes=scratch,
        compiler_params=pltpu.CompilerParams(
            collective_id=0, has_side_effects=True, vmem_limit_bytes=VMEM_BYTES
        ),
        name="interaction_layer",
    )(pooled, lc_weight, fm_proj, fm_out.T, cotangent.transpose(0, 2, 1))
    if fused:
        layer, emb, lc_g, proj_g, out_t = pl.pallas_call(
            write_kernel,
            out_shape=(
                layer_shape,
                emb_shape,
                jax.ShapeDtypeStruct((jq, n), F32),
                jax.ShapeDtypeStruct((n, kq), F32),
                jax.ShapeDtypeStruct((d, kq), F32),
            ),
            in_specs=[hbm] * 3,
            out_specs=(hbm,) * 5,
            scratch_shapes=[
                pltpu.VMEM(layer_shape.shape, BF16),
                pltpu.VMEM(emb_shape.shape, BF16),
                pltpu.VMEM(grad_shapes[0].shape, BF16),
                pltpu.VMEM((jq, n), F32),
                pltpu.VMEM((n, kq), F32),
                pltpu.VMEM((d, kq), F32),
                dma((2, 11)),
            ],
            compiler_params=pltpu.CompilerParams(vmem_limit_bytes=VMEM_BYTES),
            name="write_outputs",
        )(layer, emb, *grads)
    else:
        lc_g, proj_g, out_t = lax.psum(tuple(grads), ("rep", "table"))
    return layer.transpose(0, 2, 1), emb, lc_g, proj_g, out_t.T


def solution(mesh):
    in_specs = (
        P("rep", "table", None),
        P("tensor", None),
        P(None, "tensor"),
        P("tensor", None),
        P(("rep", "table"), None, None),
    )
    out_specs = (
        P(("rep", "table"), None, None),
        P("rep", "table", "tensor"),
        P("tensor", None),
        P(None, "tensor"),
        P("tensor", None),
    )
    return jax.shard_map(
        functools.partial(shards, dict(mesh.shape)),
        mesh=mesh, in_specs=in_specs, out_specs=out_specs, check_vma=False,
    )
```

```python
import functools

import jax
import jax.numpy as jnp
from jax import lax
from jax.experimental import pallas as pl
from jax.experimental.pallas import tpu as pltpu
from jax.sharding import PartitionSpec as P

MESH = pl.DeviceIdType.MESH
BF16 = jnp.bfloat16
F32 = jnp.float32
VMEM_BYTES = 60 * 1024 * 1024


def dot_nn(a, b):
    return jnp.dot(a, b, preferred_element_type=F32)


def dot_nt(a, b):
    return lax.dot_general(a, b, (((1,), (1,)), ((), ())), preferred_element_type=F32)


def layer_kernel(cfg, pooled, lc_w, proj_w, out_w, cot, layer, emb, *rest):
    tables, reps, tensors = cfg["tables"], cfg["reps"], cfg["tensors"]
    samples, nr, n, d = cfg["samples"], cfg["nr"], cfg["n"], cfg["d"]
    kq, jq, dq, cs, pp, fused = cfg["kq"], cfg["jq"], cfg["dq"], cfg["cs"], cfg["pp"], cfg["fused"]
    grads, scratch = (rest[:1], rest[1:]) if fused else (rest[:3], rest[3:])
    (x_ref, gt_ref, g_ref, pw, ww, ow, p_rel, ot_rel, o_rel, w_t, back, c_ref, cg_ref, i_ref, ig_ref, lo, eg, acc_l, acc_p, acc_o,
     gb, rb1, sb, rb2, fs, loc, x_send, x_recv, w_send, w_recv, f_send, f_recv, c_send, c_recv, e_send, e_recv, r_send, r_recv) = scratch
    chunks, k = samples // cs, tensors * kq
    t = lax.axis_index("table")
    r = lax.axis_index("rep")
    x = lax.axis_index("tensor")

    def peer(axis, me, size, j):
        return {axis: lax.rem(me + j, size)}

    barrier = pltpu.get_barrier_semaphore()
    groups = [("table", t, tables), ("tensor", x, tensors)] + ([("rep", r, reps)] if fused else [])
    signals = 0
    for axis, me, size in groups:
        for j in range(1, size):
            pl.semaphore_signal(barrier, inc=1, device_id=peer(axis, me, size, j), device_id_type=MESH)
            signals += 1

    g_load = pltpu.make_async_copy(cot, gt_ref, loc.at[4])

    x_load = pltpu.make_async_copy(pooled.at[pl.ds(t * samples, samples)], x_ref.at[:, t], loc.at[0])

    w_pairs = ((proj_w, pw), (out_w, ow), (lc_w, ww))
    w_loads = [
        pltpu.make_async_copy(src, dst.at[x], loc.at[1 + i]) for i, (src, dst) in enumerate(w_pairs)
    ]
    for load in w_loads:
        load.start()
    g_load.start()
    x_load.start()
    pl.semaphore_wait(barrier, signals)

    chips, rounds = tables // 2, chunks // tensors
    chip, core = t // 2, lax.rem(t, 2)
    mate = chip * 2 + lax.rem(core + 1, 2)

    c_copy = pltpu.make_async_remote_copy(
        pooled.at[pl.ds(mate * samples, samples)], x_ref.at[:, t], c_send, c_recv,
        device_id={"table": mate}, device_id_type=MESH,
    )

    def x_copy(g, a, b):
        to = lax.rem(chip + a, chips) * 2 + lax.rem(core + b, 2)
        first_row = (g * tensors + x) * cs
        return pltpu.make_async_remote_copy(
            pooled.at[pl.ds(to * samples + first_row, cs)],
            x_ref.at[pl.ds(first_row, cs), t],
            x_send.at[g, a - 1, b],
            x_recv.at[g, a - 1, b],
            device_id={"table": to},
            device_id_type=MESH,
        )

    def f_copy(g, a, j):
        source = lax.rem(chip + chips - a, chips) * 2
        held = x_ref.at[pl.ds((g * tensors + x) * cs, cs), pl.ds(source, 2)]
        return pltpu.make_async_remote_copy(
            held, held, f_send.at[g, a - 1, j - 1], f_recv.at[g, a - 1, j - 1],
            device_id=peer("tensor", x, tensors, j), device_id_type=MESH,
        )

    def pass_on(g):
        for a in range(1, chips):
            for b in range(2):
                x_copy(g, a, b).wait_recv()
            for j in range(1, tensors):
                f_copy(g, a, j).start()

    def w_copy(i, j):
        src, dst = w_pairs[i]
        return pltpu.make_async_remote_copy(
            src, dst.at[x], w_send.at[i, j - 1], w_recv.at[i, j - 1],
            device_id=peer("tensor", x, tensors, j), device_id_type=MESH,
        )

    for j in range(1, tensors):
        for i in range(3):
            w_copy(i, j).start()
    for g in range(rounds):
        for a in range(1, chips):
            for b in range(2):
                x_copy(g, a, b).start()
    c_copy.start()

    acc_l[...] = jnp.zeros_like(acc_l)
    acc_p[...] = jnp.zeros_like(acc_p)
    acc_o[...] = jnp.zeros_like(acc_o)
    g_load.wait()
    for s in range(samples):
        g_ref[s] = gt_ref[s].T
    for load in w_loads:
        load.wait()
    for j in range(1, tensors):
        for i in range(2):
            w_copy(i, j).wait_recv()
    order = [x] + [lax.rem(x + j, tensors) for j in range(1, tensors)]
    p_rel[...] = jnp.concatenate([pw[q] for q in order], axis=1)
    ot_rel[...] = jnp.concatenate([ow[q] for q in order], axis=1)
    o_rel[...] = ot_rel[...].T
    back[:k] = p_rel[...].T

    def before(c, carry):
        rows = pl.ds(c * cs, cs)
        igrad = dot_nn(g_ref[rows].reshape(cs * n, d), ot_rel[...])
        ig_ref[rows] = igrad.astype(BF16).reshape(cs, n, k)
        return carry

    lax.fori_loop(0, chunks, before, 0)

    def first(c):
        at = [c * cs + i for i in range(cs)]
        own_rows = [x_ref[s, pl.ds(x * (jq // nr), jq // nr)].reshape(jq, d) for s in at]
        xs = [x_ref[s].reshape(n, d) for s in at]
        xt = [v.T for v in xs]
        comp = dot_nn(jnp.concatenate(xt, axis=0), p_rel[...]).astype(BF16)
        comp = [comp[i * d:(i + 1) * d] for i in range(cs)]
        cgrad = [dot_nn(v, ig_ref[s]).astype(BF16) for s, v in zip(at, xt)]
        sum_l = acc_l[...]
        for s, v in zip(at, own_rows):
            sum_l = sum_l + dot_nn(v, gt_ref[s])
        inter = [dot_nn(v, w).astype(BF16) for v, w in zip(xs, comp)]
        sum_p = acc_p[...]
        for v, w in zip(xs, cgrad):
            sum_p = sum_p + dot_nn(v, w[:, :kq])
        sum_o = acc_o[:d]
        for s, v in zip(at, inter):
            sum_o = sum_o + dot_nn(gt_ref[s], v[:, :kq])
        acc_l[...] = sum_l
        acc_p[...] = sum_p
        acc_o[:d] = sum_o
        for i, s in enumerate(at):
            c_ref[s] = comp[i]
            cg_ref[s] = cgrad[i]
            i_ref[s] = inter[i]

    x_load.wait()
    c_copy.wait_recv()
    pass_on(0)
    for g in range(rounds):
        first(g * tensors + x)
        if g + 1 < rounds:
            pass_on(g + 1)
        for j in range(1, tensors):
            for a in range(1, chips):
                f_copy(g, a, j).wait_recv()
            first(g * tensors + lax.rem(x + tensors - j, tensors))

    part = reps * pp

    def rs_table(j):
        to = lax.rem(t + j, tables)
        return pltpu.make_async_remote_copy(
            gb.at[pl.ds(to * part, part)], rb1.at[j - 1], r_send.at[0, j - 1], r_recv.at[0, j - 1],
            device_id=peer("table", t, tables, j), device_id_type=MESH,
        )

    def rs_rep(j):
        to = lax.rem(r + j, reps)
        return pltpu.make_async_remote_copy(
            sb.at[pl.ds(to * pp, pp)], rb2.at[j - 1], r_send.at[1, j - 1], r_recv.at[1, j - 1],
            device_id=peer("rep", r, reps, j), device_id_type=MESH,
        )

    def ag_rep(j):
        mine = fs.at[pl.ds(t * part + r * pp, pp)]
        return pltpu.make_async_remote_copy(
            mine, mine, r_send.at[2, j - 1], r_recv.at[2, j - 1],
            device_id=peer("rep", r, reps, j), device_id_type=MESH,
        )

    def ag_table(j):
        mine = fs.at[pl.ds(t * part, part)]
        return pltpu.make_async_remote_copy(
            mine, mine, r_send.at[3, j - 1], r_recv.at[3, j - 1],
            device_id=peer("table", t, tables, j), device_id_type=MESH,
        )

    layout = ((acc_l, cfg["wide_scale"]), (acc_p, cfg["wide_scale"]), (acc_o, cfg["out_scale"]))
    if fused:
        at = 0
        for ref, scale in layout:
            rows = ref.shape[0]
            for h in range(ref.shape[1] // 128):
                value = (ref[:, h * 128:(h + 1) * 128] * scale).astype(BF16)
                gb[at:at + rows // 16] = value.reshape(rows // 16, 16, 128)
                at += rows // 16
        for j in range(1, tables):
            rs_table(j).start()

    def reduce_step(c):
        if not fused:
            return

        if c == 0:
            total = gb[pl.ds(t * part, part)].astype(F32)
            for j in range(1, tables):
                rs_table(j).wait_recv()
                total = total + rb1[j - 1].astype(F32)
            sb[...] = total.astype(BF16)
            for j in range(1, reps):
                rs_rep(j).start()

        if c == 1:
            total = sb[pl.ds(r * pp, pp)].astype(F32)
            for j in range(1, reps):
                rs_rep(j).wait_recv()
                total = total + rb2[j - 1].astype(F32)
            fs[pl.ds(t * part + r * pp, pp)] = total.astype(BF16)
            for j in range(1, reps):
                ag_rep(j).start()

        if c == 2:
            for j in range(1, reps):
                ag_rep(j).wait_recv()
            for j in range(1, tables):
                ag_table(j).start()

    for j in range(1, tensors):
        w_copy(2, j).wait_recv()
    w_t[...] = ww[...].reshape(n, n).T
    back[k:] = w_t[...]
    own_d = pl.ds(pl.multiple_of(x * dq, dq), dq)

    def lo_store(c):
        rows = pl.ds(c * cs, cs)
        return pltpu.make_async_copy(lo.at[rows], layer.at[rows], loc.at[5 + c])

    def e_store(c):
        return pltpu.make_async_copy(
            eg.at[pl.ds(c * cs, cs), t], emb.at[pl.ds(t * samples + c * cs, cs)], loc.at[5 + chunks + c]
        )

    def e_copy(c, j):
        to = lax.rem(t + j, tables)
        return pltpu.make_async_remote_copy(
            eg.at[pl.ds(c * cs, cs), to],
            emb.at[pl.ds(t * samples + c * cs, cs)],
            e_send.at[c, j - 1],
            e_recv.at[c, j - 1],
            device_id=peer("table", t, tables, j),
            device_id_type=MESH,
        )

    def second(c):
        at = [c * cs + i for i in range(cs)]
        rows = pl.ds(c * cs, cs)
        gt = gt_ref[rows, own_d]
        left = jnp.concatenate([cg_ref[rows, own_d].reshape(cs * dq, k), gt.reshape(cs * dq, n)], axis=1)
        shared = dot_nn(left, back[...]) + gt.astype(F32).reshape(cs * dq, n)
        terms = [dot_nt(c_ref[s, own_d], ig_ref[s]) for s in at]
        for i, s in enumerate(at):
            grad = shared[i * dq:(i + 1) * dq] + terms[i]
            eg[s] = grad.T.reshape(tables, nr, dq).astype(BF16)
        for j in range(1, tables):
            e_copy(c, j).start()
        e_store(c).start()

    def third(c):
        at = [c * cs + i for i in range(cs)]
        rows = pl.ds(c * cs, cs)
        mixture = dot_nn(i_ref[rows].reshape(cs * n, k), o_rel[...])
        xs = [x_ref[s].reshape(n, d) for s in at]
        mixed = [dot_nn(w_t[...], v) for v in xs]
        for i, s in enumerate(at):
            out = xs[i].astype(F32) + (mixture[i * n:(i + 1) * n] + mixed[i])
            lo[s] = out.astype(BF16).T
        lo_store(c).start()

    steps = [functools.partial(part, c) for part in (second, third) for c in range(chunks)]
    for i, step in enumerate(steps):
        step()
        reduce_step(i)

    if fused:
        for j in range(1, tables):
            ag_table(j).wait_recv()
        grads[0][...] = fs[...]
    else:
        for ref, (acc, scale) in zip(grads, layout):
            ref[...] = acc[:ref.shape[0]] * scale

    for c in range(chunks):
        lo_store(c).wait()
        e_store(c).wait()
        for j in range(1, tables):
            e_copy(c, j).wait_recv()
    for c in range(chunks):
        for j in range(1, tables):
            e_copy(c, j).wait_send()
    c_copy.wait_send()
    for g in range(rounds):
        for a in range(1, chips):
            for b in range(2):
                x_copy(g, a, b).wait_send()
            for j in range(1, tensors):
                f_copy(g, a, j).wait_send()
    for j in range(1, tensors):
        for i in range(3):
            w_copy(i, j).wait_send()
    if fused:
        for j in range(1, tables):
            rs_table(j).wait_send()
            ag_table(j).wait_send()
        for j in range(1, reps):
            rs_rep(j).wait_send()
            ag_rep(j).wait_send()


def write_kernel(layer, emb, pieces, layer_out, emb_out, lc_g, proj_g, out_g,
                 held_l, held_e, held_g, lc_v, proj_v, out_v, sems):
    g_load = pltpu.make_async_copy(pieces, held_g, sems.at[0, 8])
    g_load.start()
    loads, stores = [], []
    for src, held, dst in ((layer, held_l, layer_out), (emb, held_e, emb_out)):
        parts = 4 if src.shape[0] % 4 == 0 else 1
        size = src.shape[0] // parts
        for p in range(parts):
            rows = pl.ds(p * size, size)
            at = len(loads)
            loads.append(pltpu.make_async_copy(src.at[rows], held.at[rows], sems.at[0, at]))
            stores.append(pltpu.make_async_copy(held.at[rows], dst.at[rows], sems.at[1, at]))
    for load in loads:
        load.start()
    g_load.wait()
    at = 0
    for ref, rows in ((lc_v, lc_v.shape[0]), (proj_v, proj_v.shape[0]), (out_v, out_v.shape[0])):
        padded = -(-rows // 128) * 128
        for h in range(ref.shape[1] // 128):
            ref[:, h * 128:(h + 1) * 128] = held_g[at:at + rows // 16].reshape(rows, 128).astype(F32)
            at += padded // 16
    for i, (held, dst) in enumerate(((lc_v, lc_g), (proj_v, proj_g), (out_v, out_g))):
        stores.append(pltpu.make_async_copy(held, dst, sems.at[1, 8 + i]))
        stores[-1].start()
    for load, store in zip(loads, stores):
        load.wait()
        store.start()
    for store in stores:
        store.wait()


def shards(sizes, pooled, lc_weight, fm_proj, fm_out, cotangent):
    tables, reps, tensors = sizes["table"], sizes["rep"], sizes["tensor"]
    samples, n, d = cotangent.shape
    nr = pooled.shape[1]
    jq, kq, dq = lc_weight.shape[0], fm_out.shape[0], d // tensors
    total = samples * reps * tables
    cs = max(c for c in (1, 2, 4) if samples % (c * tensors) == 0)
    chunks = samples // cs
    rounds, chips = chunks // tensors, tables // 2
    wide = -(-d // 128) * 128
    pieces = (n // 128) * (jq // 16) + (kq // 128) * (n // 16 + wide // 16)
    group = tables * reps
    fused = pieces % group == 0 and n % 128 == 0 and jq % 128 == 0 and kq % 128 == 0
    pp = pieces // group if fused else 1
    cfg = dict(
        tables=tables, reps=reps, tensors=tensors, samples=samples, nr=nr, n=n, d=d, kq=kq, jq=jq, dq=dq,
        cs=cs, pp=pp, fused=fused,
        wide_scale=float(total * d) ** (-0.5), out_scale=float(total * n * d) ** (-0.5),
    )
    part = reps * pp if fused else 1
    held = pieces if fused else 1
    dma = pltpu.SemaphoreType.DMA
    peers = max(tables - 1, 1)
    wpeers = max(tensors - 1, 1)
    rpeers = max(tables - 1, reps - 1, 1)
    k = kq * tensors
    scratch = [
        pltpu.VMEM((samples, tables, nr, d), BF16),
        pltpu.VMEM((samples, d, n), BF16),
        pltpu.VMEM((samples, n, d), BF16),
        pltpu.VMEM((tensors, n, kq), BF16),
        pltpu.VMEM((tensors, jq, n), BF16),
        pltpu.VMEM((tensors, d, kq), BF16),
        pltpu.VMEM((n, k), BF16),
        pltpu.VMEM((d, k), BF16),
        pltpu.VMEM((k, d), BF16),
        pltpu.VMEM((n, n), BF16),
        pltpu.VMEM((k + n, n), BF16),
        pltpu.VMEM((samples, d, k), BF16),
        pltpu.VMEM((samples, d, k), BF16),
        pltpu.VMEM((samples, n, k), BF16),
        pltpu.VMEM((samples, n, k), BF16),
        pltpu.VMEM((samples, d, n), BF16),
        pltpu.VMEM((samples, tables, nr, dq), BF16),
        pltpu.VMEM((jq, n), F32),
        pltpu.VMEM((n, kq), F32),
        pltpu.VMEM((wide, kq), F32),
        pltpu.VMEM((held, 16, 128), BF16),
        pltpu.VMEM((peers, part, 16, 128), BF16),
        pltpu.VMEM((part, 16, 128), BF16),
        pltpu.VMEM((max(reps - 1, 1), pp, 16, 128), BF16),
        pltpu.VMEM((held, 16, 128), BF16),
        dma((2 * chunks + 5,)),
        dma((rounds, max(chips - 1, 1), 2)),
        dma((rounds, max(chips - 1, 1), 2)),
        dma((3, wpeers)),
        dma((3, wpeers)),
        dma((rounds, max(chips - 1, 1), wpeers)),
        dma((rounds, max(chips - 1, 1), wpeers)),
        dma,
        dma,
        dma((chunks, peers)),
        dma((chunks, peers)),
        dma((4, rpeers)),
        dma((4, rpeers)),
    ]
    hbm = pl.BlockSpec(memory_space=pl.ANY)
    vmem = pl.BlockSpec(memory_space=pltpu.VMEM)
    layer_shape = jax.ShapeDtypeStruct((samples, d, n), BF16)
    emb_shape = jax.ShapeDtypeStruct((pooled.shape[0], nr, dq), BF16)
    if fused:
        grad_shapes = (jax.ShapeDtypeStruct((pieces, 16, 128), BF16),)
    else:
        grad_shapes = tuple(jax.ShapeDtypeStruct(s, F32) for s in ((jq, n), (n, kq), (d, kq)))
    layer, emb, *grads = pl.pallas_call(
        functools.partial(layer_kernel, cfg),
        out_shape=(layer_shape, emb_shape, *grad_shapes),
        in_specs=[hbm] * 5,
        out_specs=(hbm, hbm) + (vmem,) * len(grad_shapes),
        scratch_shapes=scratch,
        compiler_params=pltpu.CompilerParams(
            collective_id=0, has_side_effects=True, vmem_limit_bytes=VMEM_BYTES
        ),
        name="interaction_layer",
    )(pooled, lc_weight, fm_proj, fm_out.T, cotangent.transpose(0, 2, 1))
    if fused:
        layer, emb, lc_g, proj_g, out_t = pl.pallas_call(
            write_kernel,
            out_shape=(
                layer_shape,
                emb_shape,
                jax.ShapeDtypeStruct((jq, n), F32),
                jax.ShapeDtypeStruct((n, kq), F32),
                jax.ShapeDtypeStruct((d, kq), F32),
            ),
            in_specs=[hbm] * 3,
            out_specs=(hbm,) * 5,
            scratch_shapes=[
                pltpu.VMEM(layer_shape.shape, BF16),
                pltpu.VMEM(emb_shape.shape, BF16),
                pltpu.VMEM(grad_shapes[0].shape, BF16),
                pltpu.VMEM((jq, n), F32),
                pltpu.VMEM((n, kq), F32),
                pltpu.VMEM((d, kq), F32),
                dma((2, 11)),
            ],
            compiler_params=pltpu.CompilerParams(vmem_limit_bytes=VMEM_BYTES),
            name="write_outputs",
        )(layer, emb, *grads)
    else:
        lc_g, proj_g, out_t = lax.psum(tuple(grads), ("rep", "table"))
    return layer.transpose(0, 2, 1), emb, lc_g, proj_g, out_t.T


def solution(mesh):
    in_specs = (
        P("rep", "table", None),
        P("tensor", None),
        P(None, "tensor"),
        P("tensor", None),
        P(("rep", "table"), None, None),
    )
    out_specs = (
        P(("rep", "table"), None, None),
        P("rep", "table", "tensor"),
        P("tensor", None),
        P(None, "tensor"),
        P("tensor", None),
    )
    return jax.shard_map(
        functools.partial(shards, dict(mesh.shape)),
        mesh=mesh, in_specs=in_specs, out_specs=out_specs, check_vma=False,
    )
```

```python
import functools

import jax
import jax.numpy as jnp
from jax import lax
from jax.experimental import pallas as pl
from jax.experimental.pallas import tpu as pltpu
from jax.sharding import PartitionSpec as P

MESH = pl.DeviceIdType.MESH
BF16 = jnp.bfloat16
F32 = jnp.float32
VMEM_BYTES = 60 * 1024 * 1024


def dot_nn(a, b):
    return jnp.dot(a, b, preferred_element_type=F32)


def layer_kernel(cfg, pooled, lc_w, proj_w, out_w, cot, layer, emb, *rest):
    tables, reps, tensors = cfg["tables"], cfg["reps"], cfg["tensors"]
    samples, nr, n, d = cfg["samples"], cfg["nr"], cfg["n"], cfg["d"]
    kq, jq, dq, cs, pp, fused = cfg["kq"], cfg["jq"], cfg["dq"], cfg["cs"], cfg["pp"], cfg["fused"]
    grads, scratch = (rest[:1], rest[1:]) if fused else (rest[:3], rest[3:])
    (x_ref, gt_ref, g_ref, xt_ref, pw, ww, ow, p_rel, ot_rel, own_ct, own_cgt, own_it, igt, lo, eg, acc_l, acc_p, acc_o,
     gb, rb1, fs, loc, x_send, x_recv, w_send, w_recv, f_send, f_recv, c_send, c_recv, e_send, e_recv, r_send, r_recv) = scratch
    chunks = samples // cs
    t = lax.axis_index("table")
    r = lax.axis_index("rep")
    x = lax.axis_index("tensor")

    def peer(axis, me, size, j):
        return {axis: lax.rem(me + j, size)}

    barrier = pltpu.get_barrier_semaphore()
    group, place = tables * reps, r * tables + t

    def member(j):
        to = lax.rem(place + j, group)
        return to, {"rep": to // tables, "table": lax.rem(to, tables)}

    greeted = [peer("tensor", x, tensors, j) for j in range(1, tensors)]
    if fused:
        greeted += [member(j)[1] for j in range(1, group)]
    else:
        greeted += [peer("table", t, tables, j) for j in range(1, tables)]
    for device in greeted:
        pl.semaphore_signal(barrier, inc=1, device_id=device, device_id_type=MESH)

    g_load = pltpu.make_async_copy(cot, gt_ref, loc.at[chunks])

    def x_load(c):
        return pltpu.make_async_copy(
            pooled.at[pl.ds(t * samples + c * cs, cs)], x_ref.at[pl.ds(c * cs, cs), t], loc.at[c]
        )

    w_pairs = ((proj_w, pw), (out_w, ow), (lc_w, ww))
    w_loads = [
        pltpu.make_async_copy(src, dst.at[x], loc.at[chunks + 1 + i]) for i, (src, dst) in enumerate(w_pairs)
    ]
    for load in w_loads:
        load.start()
    g_load.start()
    for c in range(chunks):
        x_load(c).start()
    pl.semaphore_wait(barrier, len(greeted))

    chips, rounds = tables // 2, chunks // tensors
    chip, core = t // 2, lax.rem(t, 2)
    mate = chip * 2 + lax.rem(core + 1, 2)

    def c_copy(c):
        return pltpu.make_async_remote_copy(
            pooled.at[pl.ds(mate * samples + c * cs, cs)],
            x_ref.at[pl.ds(c * cs, cs), t],
            c_send.at[c],
            c_recv.at[c],
            device_id={"table": mate},
            device_id_type=MESH,
        )

    def x_copy(g, a, b):
        to = lax.rem(chip + a, chips) * 2 + lax.rem(core + b, 2)
        first_row = (g * tensors + x) * cs
        return pltpu.make_async_remote_copy(
            pooled.at[pl.ds(to * samples + first_row, cs)],
            x_ref.at[pl.ds(first_row, cs), t],
            x_send.at[g, a - 1, b],
            x_recv.at[g, a - 1, b],
            device_id={"table": to},
            device_id_type=MESH,
        )

    def f_copy(g, a, j):
        source = lax.rem(chip + chips - a, chips) * 2
        held = x_ref.at[pl.ds((g * tensors + x) * cs, cs), pl.ds(source, 2)]
        return pltpu.make_async_remote_copy(
            held, held, f_send.at[g, a - 1, j - 1], f_recv.at[g, a - 1, j - 1],
            device_id=peer("tensor", x, tensors, j), device_id_type=MESH,
        )

    def pass_on(g):
        for a in range(1, chips):
            for b in range(2):
                x_copy(g, a, b).wait_recv()
            for j in range(1, tensors):
                f_copy(g, a, j).start()

    def w_copy(i, j):
        src, dst = w_pairs[i]
        return pltpu.make_async_remote_copy(
            src, dst.at[x], w_send.at[i, j - 1], w_recv.at[i, j - 1],
            device_id=peer("tensor", x, tensors, j), device_id_type=MESH,
        )

    for g in range(rounds):
        for a in range(1, chips):
            for b in range(2):
                x_copy(g, a, b).start()
    for c in range(chunks):
        c_copy(c).start()
    for j in range(1, tensors):
        for i in range(3):
            w_copy(i, j).start()

    for load in w_loads:
        load.wait()
    own_pt, own_o = pw[x].T, ow[x].T
    acc_l[...] = jnp.zeros_like(acc_l)
    acc_p[...] = jnp.zeros_like(acc_p)
    acc_o[...] = jnp.zeros_like(acc_o)
    g_load.wait()

    def before(c, carry):
        at = [c * cs + i for i in range(cs)]
        for s in at:
            gt = gt_ref[s]
            g_ref[s] = gt.T
            igt[s] = dot_nn(own_o, gt).astype(BF16)
        return carry

    lax.fori_loop(0, chunks, before, 0)

    def first(c):
        at = [c * cs + i for i in range(cs)]
        own_rows = [x_ref[s, pl.ds(x * (jq // nr), jq // nr)].reshape(jq, d) for s in at]
        xs = [x_ref[s].reshape(n, d) for s in at]
        xt = [v.T for v in xs]
        comp = [dot_nn(own_pt, v).astype(BF16) for v in xs]
        cgrad = [dot_nn(igt[s], v).astype(BF16) for s, v in zip(at, xs)]
        sum_l = acc_l[...]
        for s, v in zip(at, own_rows):
            sum_l = sum_l + dot_nn(v, gt_ref[s])
        inter = [dot_nn(v, w).astype(BF16) for v, w in zip(comp, xt)]
        sum_p = acc_p[...]
        for v, w in zip(cgrad, xt):
            sum_p = sum_p + dot_nn(v, w)
        sum_o = acc_o[:, :d]
        for s, v in zip(at, inter):
            sum_o = sum_o + dot_nn(v, g_ref[s])
        acc_l[...] = sum_l
        acc_p[...] = sum_p
        acc_o[:, :d] = sum_o
        for i, s in enumerate(at):
            xt_ref[s] = xt[i]
            own_ct[s] = comp[i]
            own_cgt[s] = cgrad[i]
            own_it[s] = inter[i]

    for c in range(chunks):
        x_load(c).wait()
        c_copy(c).wait_recv()
    pass_on(0)
    for g in range(rounds):
        first(g * tensors + x)
        if g + 1 < rounds:
            pass_on(g + 1)
        for j in range(1, tensors):
            for a in range(1, chips):
                f_copy(g, a, j).wait_recv()
            first(g * tensors + lax.rem(x + tensors - j, tensors))

    def scatter(j):
        to, device = member(j)
        return pltpu.make_async_remote_copy(
            gb.at[pl.ds(to * pp, pp)], rb1.at[j - 1], r_send.at[0, j - 1], r_recv.at[0, j - 1],
            device_id=device, device_id_type=MESH,
        )

    def gather(j):
        mine = fs.at[pl.ds(place * pp, pp)]
        return pltpu.make_async_remote_copy(
            mine, mine, r_send.at[1, j - 1], r_recv.at[1, j - 1],
            device_id=member(j)[1], device_id_type=MESH,
        )

    layout = ((acc_l, jq, cfg["wide_scale"]), (acc_p, kq, cfg["wide_scale"]), (acc_o, kq, cfg["out_scale"]))
    if fused:
        at = 0
        for ref, rows, scale in layout:
            for h in range(n // 128):
                value = (ref[:, h * 128:(h + 1) * 128] * scale).astype(BF16)
                gb[at:at + rows // 16] = value.reshape(rows // 16, 16, 128)
                at += rows // 16
        for j in range(1, group):
            scatter(j).start()

    def reduce_step(c):
        if not fused:
            return

        @pl.when(c == 1)
        def _():
            total = gb[pl.ds(place * pp, pp)].astype(F32)
            for j in range(1, group):
                scatter(j).wait_recv()
                total = total + rb1[j - 1].astype(F32)
            fs[pl.ds(place * pp, pp)] = total.astype(BF16)
            for j in range(1, group):
                gather(j).start()

    for j in range(1, tensors):
        for i in range(3):
            w_copy(i, j).wait_recv()
    order = [x] + [lax.rem(x + j, tensors) for j in range(1, tensors)]
    p_rel[...] = jnp.concatenate([pw[q] for q in order], axis=1)
    ot_rel[...] = jnp.concatenate([ow[q] for q in order], axis=1)
    other_pt = [pw[q].T for q in order[1:]]
    other_o = [ow[q].T for q in order[1:]]

    def lo_store(c):
        rows = pl.ds(c * cs, cs)
        return pltpu.make_async_copy(lo.at[rows], layer.at[rows], loc.at[chunks + 4 + c])

    def e_store(c):
        return pltpu.make_async_copy(
            eg.at[pl.ds(c * cs, cs), t], emb.at[pl.ds(t * samples + c * cs, cs)], loc.at[2 * chunks + 4 + c]
        )

    def e_copy(c, j):
        to = lax.rem(t + j, tables)
        return pltpu.make_async_remote_copy(
            eg.at[pl.ds(c * cs, cs), to],
            emb.at[pl.ds(t * samples + c * cs, cs)],
            e_send.at[c, j - 1],
            e_recv.at[c, j - 1],
            device_id=peer("table", t, tables, j),
            device_id_type=MESH,
        )

    def second(c, carry):
        at = [c * cs + i for i in range(cs)]
        xs = [x_ref[s].reshape(n, d) for s in at]
        w_all = ww[...].reshape(n, n)
        igrad_t = [[dot_nn(v, gt_ref[s]).astype(BF16) for v in other_o] for s in at]
        comp = [[dot_nn(v, w).astype(BF16) for v in other_pt] for w in xs]
        igrad = [dot_nn(g_ref[s], ot_rel[...]).astype(BF16) for s in at]
        cgrad = [[dot_nn(v, w).astype(BF16) for v in vs] for vs, w in zip(igrad_t, xs)]
        inter = [[dot_nn(v, xt_ref[s]).astype(BF16) for v in vs] for vs, s in zip(comp, at)]
        for i, s in enumerate(at):
            gs = g_ref[s]
            left = jnp.concatenate([igrad[i], p_rel[...], w_all], axis=1)
            right = jnp.concatenate([own_ct[s], *comp[i], own_cgt[s], *cgrad[i], gs], axis=0)
            grad = dot_nn(left, right) + gs.astype(F32)
            own = grad[:, :dq]
            for q in range(1, tensors):
                own = jnp.where(x == q, grad[:, q * dq:(q + 1) * dq], own)
            eg[s] = own.reshape(tables, nr, dq).astype(BF16)
        for j in range(1, tables):
            e_copy(c, j).start()
        e_store(c).start()
        for i, s in enumerate(at):
            xt = xt_ref[s]
            left = jnp.concatenate([ot_rel[...], xt], axis=1)
            right = jnp.concatenate([own_it[s], *inter[i], w_all], axis=0)
            lo[s] = (dot_nn(left, right) + xt.astype(F32)).astype(BF16)
        lo_store(c).start()
        reduce_step(c)
        return carry

    lax.fori_loop(0, chunks, second, 0)

    if fused:
        for j in range(1, group):
            gather(j).wait_recv()
        grads[0][...] = fs[...]
    else:
        for ref, (acc, rows, scale) in zip(grads, layout):
            ref[...] = acc[:, :ref.shape[1]] * scale

    for c in range(chunks):
        lo_store(c).wait()
        e_store(c).wait()
        for j in range(1, tables):
            e_copy(c, j).wait_recv()
    for c in range(chunks):
        c_copy(c).wait_send()
        for j in range(1, tables):
            e_copy(c, j).wait_send()
    for g in range(rounds):
        for a in range(1, chips):
            for b in range(2):
                x_copy(g, a, b).wait_send()
            for j in range(1, tensors):
                f_copy(g, a, j).wait_send()
    for j in range(1, tensors):
        for i in range(3):
            w_copy(i, j).wait_send()
    if fused:
        for j in range(1, group):
            scatter(j).wait_send()
            gather(j).wait_send()


def write_kernel(layer, emb, pieces, layer_out, emb_out, lc_g, proj_g, out_g,
                 held_l, held_e, held_g, lc_v, proj_v, out_v, sems):
    g_load = pltpu.make_async_copy(pieces, held_g, sems.at[0, 8])
    g_load.start()
    loads, stores = [], []
    for src, held, dst in ((layer, held_l, layer_out), (emb, held_e, emb_out)):
        parts = 4 if src.shape[0] % 4 == 0 else 1
        size = src.shape[0] // parts
        for p in range(parts):
            rows = pl.ds(p * size, size)
            at = len(loads)
            loads.append(pltpu.make_async_copy(src.at[rows], held.at[rows], sems.at[0, at]))
            stores.append(pltpu.make_async_copy(held.at[rows], dst.at[rows], sems.at[1, at]))
    for load in loads:
        load.start()
    g_load.wait()
    at = 0
    wide = []
    for rows in (lc_g.shape[0], proj_g.shape[1], out_g.shape[1]):
        halves = []
        for _ in range(lc_g.shape[1] // 128):
            halves.append(held_g[at:at + rows // 16].reshape(rows, 128).astype(F32))
            at += rows // 16
        wide.append(halves)
    lc_v[...] = jnp.concatenate(wide[0], axis=1)
    proj_v[...] = jnp.concatenate([half.T for half in wide[1]], axis=0)
    out_v[...] = jnp.concatenate([half.T for half in wide[2]], axis=0)[:out_g.shape[0]]
    for i, (held, dst) in enumerate(((lc_v, lc_g), (proj_v, proj_g), (out_v, out_g))):
        stores.append(pltpu.make_async_copy(held, dst, sems.at[1, 8 + i]))
        stores[-1].start()
    for load, store in zip(loads, stores):
        load.wait()
        store.start()
    for store in stores:
        store.wait()


def shards(sizes, pooled, lc_weight, fm_proj, fm_out, cotangent):
    tables, reps, tensors = sizes["table"], sizes["rep"], sizes["tensor"]
    samples, n, d = cotangent.shape
    nr = pooled.shape[1]
    jq, kq, dq = lc_weight.shape[0], fm_out.shape[0], d // tensors
    total = samples * reps * tables
    cs = 2 if samples % (2 * tensors) == 0 else 1
    chunks = samples // cs
    rounds, chips = chunks // tensors, tables // 2
    wide = -(-d // 128) * 128
    pieces = (n // 128) * (jq // 16 + kq // 16) + (wide // 128) * (kq // 16)
    group = tables * reps
    fused = pieces % group == 0 and wide == n and jq % 16 == 0 and kq % 16 == 0
    pp = pieces // group if fused else 1
    cfg = dict(
        tables=tables, reps=reps, tensors=tensors, samples=samples, nr=nr, n=n, d=d, kq=kq, jq=jq, dq=dq,
        cs=cs, pp=pp, fused=fused,
        wide_scale=float(total * d) ** (-0.5), out_scale=float(total * n * d) ** (-0.5),
    )
    held = pieces if fused else 1
    dma = pltpu.SemaphoreType.DMA
    peers = max(tables - 1, 1)
    wpeers = max(tensors - 1, 1)
    rpeers = max(group - 1, 1) if fused else 1
    k = kq * tensors
    scratch = [
        pltpu.VMEM((samples, tables, nr, d), BF16),
        pltpu.VMEM((samples, d, n), BF16),
        pltpu.VMEM((samples, n, d), BF16),
        pltpu.VMEM((samples, d, n), BF16),
        pltpu.VMEM((tensors, n, kq), BF16),
        pltpu.VMEM((tensors, jq, n), BF16),
        pltpu.VMEM((tensors, d, kq), BF16),
        pltpu.VMEM((n, k), BF16),
        pltpu.VMEM((d, k), BF16),
        pltpu.VMEM((samples, kq, d), BF16),
        pltpu.VMEM((samples, kq, d), BF16),
        pltpu.VMEM((samples, kq, n), BF16),
        pltpu.VMEM((samples, kq, n), BF16),
        pltpu.VMEM((samples, d, n), BF16),
        pltpu.VMEM((samples, tables, nr, dq), BF16),
        pltpu.VMEM((jq, n), F32),
        pltpu.VMEM((kq, n), F32),
        pltpu.VMEM((kq, wide), F32),
        pltpu.VMEM((held, 16, 128), BF16),
        pltpu.VMEM((rpeers, pp, 16, 128), BF16),
        pltpu.VMEM((held, 16, 128), BF16),
        dma((3 * chunks + 4,)),
        dma((rounds, max(chips - 1, 1), 2)),
        dma((rounds, max(chips - 1, 1), 2)),
        dma((3, wpeers)),
        dma((3, wpeers)),
        dma((rounds, max(chips - 1, 1), wpeers)),
        dma((rounds, max(chips - 1, 1), wpeers)),
        dma((chunks,)),
        dma((chunks,)),
        dma((chunks, peers)),
        dma((chunks, peers)),
        dma((2, rpeers)),
        dma((2, rpeers)),
    ]
    hbm = pl.BlockSpec(memory_space=pl.ANY)
    vmem = pl.BlockSpec(memory_space=pltpu.VMEM)
    layer_shape = jax.ShapeDtypeStruct((samples, d, n), BF16)
    emb_shape = jax.ShapeDtypeStruct((pooled.shape[0], nr, dq), BF16)
    if fused:
        grad_shapes = (jax.ShapeDtypeStruct((pieces, 16, 128), BF16),)
    else:
        grad_shapes = tuple(jax.ShapeDtypeStruct(s, F32) for s in ((jq, n), (kq, n), (kq, d)))
    layer, emb, *grads = pl.pallas_call(
        functools.partial(layer_kernel, cfg),
        out_shape=(layer_shape, emb_shape, *grad_shapes),
        in_specs=[hbm] * 5,
        out_specs=(hbm, hbm) + (vmem,) * len(grad_shapes),
        scratch_shapes=scratch,
        compiler_params=pltpu.CompilerParams(
            collective_id=0, has_side_effects=True, vmem_limit_bytes=VMEM_BYTES
        ),
        name="interaction_layer",
    )(pooled, lc_weight, fm_proj, fm_out.T, cotangent.transpose(0, 2, 1))
    if fused:
        layer, emb, lc_g, proj_g, out_t = pl.pallas_call(
            write_kernel,
            out_shape=(
                layer_shape,
                emb_shape,
                jax.ShapeDtypeStruct((jq, n), F32),
                jax.ShapeDtypeStruct((n, kq), F32),
                jax.ShapeDtypeStruct((d, kq), F32),
            ),
            in_specs=[hbm] * 3,
            out_specs=(hbm,) * 5,
            scratch_shapes=[
                pltpu.VMEM(layer_shape.shape, BF16),
                pltpu.VMEM(emb_shape.shape, BF16),
                pltpu.VMEM(grad_shapes[0].shape, BF16),
                pltpu.VMEM((jq, n), F32),
                pltpu.VMEM((n, kq), F32),
                pltpu.VMEM((d, kq), F32),
                dma((2, 11)),
            ],
            compiler_params=pltpu.CompilerParams(vmem_limit_bytes=VMEM_BYTES),
            name="write_outputs",
        )(layer, emb, *grads)
        out_g = out_t.T
    else:
        lc_g, proj_t, out_g = lax.psum(tuple(grads), ("rep", "table"))
        proj_g = proj_t.T
    return layer.transpose(0, 2, 1), emb, lc_g, proj_g, out_g


def solution(mesh):
    in_specs = (
        P("rep", "table", None),
        P("tensor", None),
        P(None, "tensor"),
        P("tensor", None),
        P(("rep", "table"), None, None),
    )
    out_specs = (
        P(("rep", "table"), None, None),
        P("rep", "table", "tensor"),
        P("tensor", None),
        P(None, "tensor"),
        P("tensor", None),
    )
    return jax.shard_map(
        functools.partial(shards, dict(mesh.shape)),
        mesh=mesh, in_specs=in_specs, out_specs=out_specs, check_vma=False,
    )
```

```python
import functools

import jax
import jax.numpy as jnp
from jax import lax
from jax.experimental import pallas as pl
from jax.experimental.pallas import tpu as pltpu
from jax.sharding import PartitionSpec as P

MESH = pl.DeviceIdType.MESH
BF16 = jnp.bfloat16
F32 = jnp.float32
VMEM_BYTES = 60 * 1024 * 1024


def dot_nn(a, b):
    return jnp.dot(a, b, preferred_element_type=F32)


def layer_kernel(cfg, pooled, lc_w, proj_w, out_w, cot, layer, emb, *rest):
    tables, reps, tensors = cfg["tables"], cfg["reps"], cfg["tensors"]
    samples, nr, n, d = cfg["samples"], cfg["nr"], cfg["n"], cfg["d"]
    kq, jq, dq, cs, pp, fused = cfg["kq"], cfg["jq"], cfg["dq"], cfg["cs"], cfg["pp"], cfg["fused"]
    grads, scratch = (rest[:1], rest[1:]) if fused else (rest[:3], rest[3:])
    (x_ref, gt_ref, g_ref, xt_ref, pw, ww, ow, p_rel, ot_rel, own_ct, own_cgt, own_it, igt, lo, eg, acc_l, acc_p, acc_o,
     gb, rb1, fs, loc, x_send, x_recv, w_send, w_recv, f_send, f_recv, c_send, c_recv, e_send, e_recv, r_send, r_recv) = scratch
    chunks = samples // cs
    t = lax.axis_index("table")
    r = lax.axis_index("rep")
    x = lax.axis_index("tensor")

    def peer(axis, me, size, j):
        return {axis: lax.rem(me + j, size)}

    barrier = pltpu.get_barrier_semaphore()
    group, place = tables * reps, r * tables + t

    def member(j):
        to = lax.rem(place + j, group)
        return to, {"rep": to // tables, "table": lax.rem(to, tables)}

    greeted = [peer("tensor", x, tensors, j) for j in range(1, tensors)]
    if fused:
        greeted += [member(j)[1] for j in range(1, group)]
    else:
        greeted += [peer("table", t, tables, j) for j in range(1, tables)]
    for device in greeted:
        pl.semaphore_signal(barrier, inc=1, device_id=device, device_id_type=MESH)

    g_load = pltpu.make_async_copy(cot, gt_ref, loc.at[chunks])

    def x_load(c):
        return pltpu.make_async_copy(
            pooled.at[pl.ds(t * samples + c * cs, cs)], x_ref.at[pl.ds(c * cs, cs), t], loc.at[c]
        )

    w_pairs = ((proj_w, pw), (out_w, ow), (lc_w, ww))
    w_loads = [
        pltpu.make_async_copy(src, dst.at[x], loc.at[chunks + 1 + i]) for i, (src, dst) in enumerate(w_pairs)
    ]
    for load in w_loads:
        load.start()
    g_load.start()
    for c in range(chunks):
        x_load(c).start()
    pl.semaphore_wait(barrier, len(greeted))

    chips, rounds = tables // 2, chunks // tensors
    chip, core = t // 2, lax.rem(t, 2)
    mate = chip * 2 + lax.rem(core + 1, 2)

    def c_copy(c):
        return pltpu.make_async_remote_copy(
            pooled.at[pl.ds(mate * samples + c * cs, cs)],
            x_ref.at[pl.ds(c * cs, cs), t],
            c_send.at[c],
            c_recv.at[c],
            device_id={"table": mate},
            device_id_type=MESH,
        )

    def x_copy(g, a, b):
        to = lax.rem(chip + a, chips) * 2 + lax.rem(core + b, 2)
        first_row = (g * tensors + x) * cs
        return pltpu.make_async_remote_copy(
            pooled.at[pl.ds(to * samples + first_row, cs)],
            x_ref.at[pl.ds(first_row, cs), t],
            x_send.at[g, a - 1, b],
            x_recv.at[g, a - 1, b],
            device_id={"table": to},
            device_id_type=MESH,
        )

    def f_copy(g, a, j):
        source = lax.rem(chip + chips - a, chips) * 2
        held = x_ref.at[pl.ds((g * tensors + x) * cs, cs), pl.ds(source, 2)]
        return pltpu.make_async_remote_copy(
            held, held, f_send.at[g, a - 1, j - 1], f_recv.at[g, a - 1, j - 1],
            device_id=peer("tensor", x, tensors, j), device_id_type=MESH,
        )

    def pass_on(g):
        for a in range(1, chips):
            for b in range(2):
                x_copy(g, a, b).wait_recv()
            for j in range(1, tensors):
                f_copy(g, a, j).start()
        if g == rounds - 1:
            for j in range(1, tensors):
                for i in range(3):
                    w_copy(i, j).start()

    def w_copy(i, j):
        src, dst = w_pairs[i]
        return pltpu.make_async_remote_copy(
            src, dst.at[x], w_send.at[i, j - 1], w_recv.at[i, j - 1],
            device_id=peer("tensor", x, tensors, j), device_id_type=MESH,
        )

    for g in range(rounds):
        for a in range(1, chips):
            for b in range(2):
                x_copy(g, a, b).start()
    for c in range(chunks):
        c_copy(c).start()

    for load in w_loads:
        load.wait()
    own_pt, own_o = pw[x].T, ow[x].T
    acc_l[...] = jnp.zeros_like(acc_l)
    acc_p[...] = jnp.zeros_like(acc_p)
    acc_o[...] = jnp.zeros_like(acc_o)
    g_load.wait()

    def before(c, carry):
        at = [c * cs + i for i in range(cs)]
        for s in at:
            gt = gt_ref[s]
            g_ref[s] = gt.T
            igt[s] = dot_nn(own_o, gt).astype(BF16)
        return carry

    lax.fori_loop(0, chunks, before, 0)

    def first(c):
        at = [c * cs + i for i in range(cs)]
        own_rows = [x_ref[s, pl.ds(x * (jq // nr), jq // nr)].reshape(jq, d) for s in at]
        xs = [x_ref[s].reshape(n, d) for s in at]
        xt = [v.T for v in xs]
        comp = [dot_nn(own_pt, v).astype(BF16) for v in xs]
        cgrad = [dot_nn(igt[s], v).astype(BF16) for s, v in zip(at, xs)]
        sum_l = acc_l[...]
        for s, v in zip(at, own_rows):
            sum_l = sum_l + dot_nn(v, gt_ref[s])
        inter = [dot_nn(v, w).astype(BF16) for v, w in zip(comp, xt)]
        sum_p = acc_p[...]
        for v, w in zip(cgrad, xt):
            sum_p = sum_p + dot_nn(v, w)
        sum_o = acc_o[:, :d]
        for s, v in zip(at, inter):
            sum_o = sum_o + dot_nn(v, g_ref[s])
        acc_l[...] = sum_l
        acc_p[...] = sum_p
        acc_o[:, :d] = sum_o
        for i, s in enumerate(at):
            xt_ref[s] = xt[i]
            own_ct[s] = comp[i]
            own_cgt[s] = cgrad[i]
            own_it[s] = inter[i]

    for c in range(chunks):
        x_load(c).wait()
        c_copy(c).wait_recv()
    pass_on(0)
    for g in range(rounds):
        first(g * tensors + x)
        if g + 1 < rounds:
            pass_on(g + 1)
        for j in range(1, tensors):
            for a in range(1, chips):
                f_copy(g, a, j).wait_recv()
            first(g * tensors + lax.rem(x + tensors - j, tensors))

    def scatter(j):
        to, device = member(j)
        return pltpu.make_async_remote_copy(
            gb.at[pl.ds(to * pp, pp)], rb1.at[j - 1], r_send.at[0, j - 1], r_recv.at[0, j - 1],
            device_id=device, device_id_type=MESH,
        )

    def gather(j):
        mine = fs.at[pl.ds(place * pp, pp)]
        return pltpu.make_async_remote_copy(
            mine, mine, r_send.at[1, j - 1], r_recv.at[1, j - 1],
            device_id=member(j)[1], device_id_type=MESH,
        )

    layout = ((acc_l, jq, cfg["wide_scale"]), (acc_p, kq, cfg["wide_scale"]), (acc_o, kq, cfg["out_scale"]))
    if fused:
        at = 0
        for ref, rows, scale in layout:
            for h in range(n // 128):
                value = (ref[:, h * 128:(h + 1) * 128] * scale).astype(BF16)
                gb[at:at + rows // 16] = value.reshape(rows // 16, 16, 128)
                at += rows // 16
        for j in range(1, group):
            scatter(j).start()

    def reduce_step(c):
        if not fused:
            return

        @pl.when(c == 1)
        def _():
            total = gb[pl.ds(place * pp, pp)].astype(F32)
            for j in range(1, group):
                scatter(j).wait_recv()
                total = total + rb1[j - 1].astype(F32)
            fs[pl.ds(place * pp, pp)] = total.astype(BF16)
            for j in range(1, group):
                gather(j).start()

    for j in range(1, tensors):
        for i in range(3):
            w_copy(i, j).wait_recv()
    order = [x] + [lax.rem(x + j, tensors) for j in range(1, tensors)]
    p_rel[...] = jnp.concatenate([pw[q] for q in order], axis=1)
    ot_rel[...] = jnp.concatenate([ow[q] for q in order], axis=1)
    other_pt = [pw[q].T for q in order[1:]]
    other_o = [ow[q].T for q in order[1:]]

    def lo_store(c):
        rows = pl.ds(c * cs, cs)
        return pltpu.make_async_copy(lo.at[rows], layer.at[rows], loc.at[chunks + 4 + c])

    def e_store(c):
        return pltpu.make_async_copy(
            eg.at[pl.ds(c * cs, cs), t], emb.at[pl.ds(t * samples + c * cs, cs)], loc.at[2 * chunks + 4 + c]
        )

    def e_copy(c, j):
        to = lax.rem(t + j, tables)
        return pltpu.make_async_remote_copy(
            eg.at[pl.ds(c * cs, cs), to],
            emb.at[pl.ds(t * samples + c * cs, cs)],
            e_send.at[c, j - 1],
            e_recv.at[c, j - 1],
            device_id=peer("table", t, tables, j),
            device_id_type=MESH,
        )

    def second(c, carry):
        at = [c * cs + i for i in range(cs)]
        xs = [x_ref[s].reshape(n, d) for s in at]
        w_all = ww[...].reshape(n, n)
        igrad_t = [[dot_nn(v, gt_ref[s]).astype(BF16) for v in other_o] for s in at]
        comp = [[dot_nn(v, w).astype(BF16) for v in other_pt] for w in xs]
        igrad = [dot_nn(g_ref[s], ot_rel[...]).astype(BF16) for s in at]
        cgrad = [[dot_nn(v, w).astype(BF16) for v in vs] for vs, w in zip(igrad_t, xs)]
        inter = [[dot_nn(v, xt_ref[s]).astype(BF16) for v in vs] for vs, s in zip(comp, at)]
        for i, s in enumerate(at):
            gs = g_ref[s]
            left = jnp.concatenate([igrad[i], p_rel[...], w_all], axis=1)
            right = jnp.concatenate([own_ct[s], *comp[i], own_cgt[s], *cgrad[i], gs], axis=0)
            grad = dot_nn(left, right) + gs.astype(F32)
            own = grad[:, :dq]
            for q in range(1, tensors):
                own = jnp.where(x == q, grad[:, q * dq:(q + 1) * dq], own)
            eg[s] = own.reshape(tables, nr, dq).astype(BF16)
        for j in range(1, tables):
            e_copy(c, j).start()
        e_store(c).start()
        for i, s in enumerate(at):
            xt = xt_ref[s]
            left = jnp.concatenate([ot_rel[...], xt], axis=1)
            right = jnp.concatenate([own_it[s], *inter[i], w_all], axis=0)
            lo[s] = (dot_nn(left, right) + xt.astype(F32)).astype(BF16)
        lo_store(c).start()
        reduce_step(c)
        return carry

    lax.fori_loop(0, chunks, second, 0)

    if fused:
        for j in range(1, group):
            gather(j).wait_recv()
        grads[0][...] = fs[...]
    else:
        for ref, (acc, rows, scale) in zip(grads, layout):
            ref[...] = acc[:, :ref.shape[1]] * scale

    for c in range(chunks):
        lo_store(c).wait()
        e_store(c).wait()
        for j in range(1, tables):
            e_copy(c, j).wait_recv()
    for c in range(chunks):
        c_copy(c).wait_send()
        for j in range(1, tables):
            e_copy(c, j).wait_send()
    for g in range(rounds):
        for a in range(1, chips):
            for b in range(2):
                x_copy(g, a, b).wait_send()
            for j in range(1, tensors):
                f_copy(g, a, j).wait_send()
    for j in range(1, tensors):
        for i in range(3):
            w_copy(i, j).wait_send()
    if fused:
        for j in range(1, group):
            scatter(j).wait_send()
            gather(j).wait_send()


def write_kernel(layer, emb, pieces, layer_out, emb_out, lc_g, proj_g, out_g,
                 held_l, held_e, held_g, lc_v, proj_v, out_v, sems):
    g_load = pltpu.make_async_copy(pieces, held_g, sems.at[0, 8])
    g_load.start()
    loads, stores = [], []
    for src, held, dst in ((layer, held_l, layer_out), (emb, held_e, emb_out)):
        parts = 4 if src.shape[0] % 4 == 0 else 1
        size = src.shape[0] // parts
        for p in range(parts):
            rows = pl.ds(p * size, size)
            at = len(loads)
            loads.append(pltpu.make_async_copy(src.at[rows], held.at[rows], sems.at[0, at]))
            stores.append(pltpu.make_async_copy(held.at[rows], dst.at[rows], sems.at[1, at]))
    for load in loads:
        load.start()
    g_load.wait()
    at = 0
    wide = []
    for rows in (lc_g.shape[0], proj_g.shape[1], out_g.shape[1]):
        halves = []
        for _ in range(lc_g.shape[1] // 128):
            halves.append(held_g[at:at + rows // 16].reshape(rows, 128).astype(F32))
            at += rows // 16
        wide.append(halves)
    lc_v[...] = jnp.concatenate(wide[0], axis=1)
    proj_v[...] = jnp.concatenate([half.T for half in wide[1]], axis=0)
    out_v[...] = jnp.concatenate([half.T for half in wide[2]], axis=0)[:out_g.shape[0]]
    for i, (held, dst) in enumerate(((lc_v, lc_g), (proj_v, proj_g), (out_v, out_g))):
        stores.append(pltpu.make_async_copy(held, dst, sems.at[1, 8 + i]))
        stores[-1].start()
    for load, store in zip(loads, stores):
        load.wait()
        store.start()
    for store in stores:
        store.wait()


def shards(sizes, pooled, lc_weight, fm_proj, fm_out, cotangent):
    tables, reps, tensors = sizes["table"], sizes["rep"], sizes["tensor"]
    samples, n, d = cotangent.shape
    nr = pooled.shape[1]
    jq, kq, dq = lc_weight.shape[0], fm_out.shape[0], d // tensors
    total = samples * reps * tables
    cs = 2 if samples % (2 * tensors) == 0 else 1
    chunks = samples // cs
    rounds, chips = chunks // tensors, tables // 2
    wide = -(-d // 128) * 128
    pieces = (n // 128) * (jq // 16 + kq // 16) + (wide // 128) * (kq // 16)
    group = tables * reps
    fused = pieces % group == 0 and wide == n and jq % 16 == 0 and kq % 16 == 0
    pp = pieces // group if fused else 1
    cfg = dict(
        tables=tables, reps=reps, tensors=tensors, samples=samples, nr=nr, n=n, d=d, kq=kq, jq=jq, dq=dq,
        cs=cs, pp=pp, fused=fused,
        wide_scale=float(total * d) ** (-0.5), out_scale=float(total * n * d) ** (-0.5),
    )
    held = pieces if fused else 1
    dma = pltpu.SemaphoreType.DMA
    peers = max(tables - 1, 1)
    wpeers = max(tensors - 1, 1)
    rpeers = max(group - 1, 1) if fused else 1
    k = kq * tensors
    scratch = [
        pltpu.VMEM((samples, tables, nr, d), BF16),
        pltpu.VMEM((samples, d, n), BF16),
        pltpu.VMEM((samples, n, d), BF16),
        pltpu.VMEM((samples, d, n), BF16),
        pltpu.VMEM((tensors, n, kq), BF16),
        pltpu.VMEM((tensors, jq, n), BF16),
        pltpu.VMEM((tensors, d, kq), BF16),
        pltpu.VMEM((n, k), BF16),
        pltpu.VMEM((d, k), BF16),
        pltpu.VMEM((samples, kq, d), BF16),
        pltpu.VMEM((samples, kq, d), BF16),
        pltpu.VMEM((samples, kq, n), BF16),
        pltpu.VMEM((samples, kq, n), BF16),
        pltpu.VMEM((samples, d, n), BF16),
        pltpu.VMEM((samples, tables, nr, dq), BF16),
        pltpu.VMEM((jq, n), F32),
        pltpu.VMEM((kq, n), F32),
        pltpu.VMEM((kq, wide), F32),
        pltpu.VMEM((held, 16, 128), BF16),
        pltpu.VMEM((rpeers, pp, 16, 128), BF16),
        pltpu.VMEM((held, 16, 128), BF16),
        dma((3 * chunks + 4,)),
        dma((rounds, max(chips - 1, 1), 2)),
        dma((rounds, max(chips - 1, 1), 2)),
        dma((3, wpeers)),
        dma((3, wpeers)),
        dma((rounds, max(chips - 1, 1), wpeers)),
        dma((rounds, max(chips - 1, 1), wpeers)),
        dma((chunks,)),
        dma((chunks,)),
        dma((chunks, peers)),
        dma((chunks, peers)),
        dma((2, rpeers)),
        dma((2, rpeers)),
    ]
    hbm = pl.BlockSpec(memory_space=pl.ANY)
    vmem = pl.BlockSpec(memory_space=pltpu.VMEM)
    layer_shape = jax.ShapeDtypeStruct((samples, d, n), BF16)
    emb_shape = jax.ShapeDtypeStruct((pooled.shape[0], nr, dq), BF16)
    if fused:
        grad_shapes = (jax.ShapeDtypeStruct((pieces, 16, 128), BF16),)
    else:
        grad_shapes = tuple(jax.ShapeDtypeStruct(s, F32) for s in ((jq, n), (kq, n), (kq, d)))
    layer, emb, *grads = pl.pallas_call(
        functools.partial(layer_kernel, cfg),
        out_shape=(layer_shape, emb_shape, *grad_shapes),
        in_specs=[hbm] * 5,
        out_specs=(hbm, hbm) + (vmem,) * len(grad_shapes),
        scratch_shapes=scratch,
        compiler_params=pltpu.CompilerParams(
            collective_id=0, has_side_effects=True, vmem_limit_bytes=VMEM_BYTES
        ),
        name="interaction_layer",
    )(pooled, lc_weight, fm_proj, fm_out.T, cotangent.transpose(0, 2, 1))
    if fused:
        layer, emb, lc_g, proj_g, out_t = pl.pallas_call(
            write_kernel,
            out_shape=(
                layer_shape,
                emb_shape,
                jax.ShapeDtypeStruct((jq, n), F32),
                jax.ShapeDtypeStruct((n, kq), F32),
                jax.ShapeDtypeStruct((d, kq), F32),
            ),
            in_specs=[hbm] * 3,
            out_specs=(hbm,) * 5,
            scratch_shapes=[
                pltpu.VMEM(layer_shape.shape, BF16),
                pltpu.VMEM(emb_shape.shape, BF16),
                pltpu.VMEM(grad_shapes[0].shape, BF16),
                pltpu.VMEM((jq, n), F32),
                pltpu.VMEM((n, kq), F32),
                pltpu.VMEM((d, kq), F32),
                dma((2, 11)),
            ],
            compiler_params=pltpu.CompilerParams(vmem_limit_bytes=VMEM_BYTES),
            name="write_outputs",
        )(layer, emb, *grads)
        out_g = out_t.T
    else:
        lc_g, proj_t, out_g = lax.psum(tuple(grads), ("rep", "table"))
        proj_g = proj_t.T
    return layer.transpose(0, 2, 1), emb, lc_g, proj_g, out_g


def solution(mesh):
    in_specs = (
        P("rep", "table", None),
        P("tensor", None),
        P(None, "tensor"),
        P("tensor", None),
        P(("rep", "table"), None, None),
    )
    out_specs = (
        P(("rep", "table"), None, None),
        P("rep", "table", "tensor"),
        P("tensor", None),
        P(None, "tensor"),
        P("tensor", None),
    )
    return jax.shard_map(
        functools.partial(shards, dict(mesh.shape)),
        mesh=mesh, in_specs=in_specs, out_specs=out_specs, check_vma=False,
    )
```
